128 devices in a mesh: comp: 4 (over y_hi, core), tile: 32 (over x, z, y_lo).
Axes of the slice: x: 4, y: 4 (y_hi: 2, y_lo: 2; y = y_hi * 2 + y_lo), z: 4, core: 2. Of those that a mesh axis runs over, the one named last changes fastest.
Arguments:
- state: float32 [4, 32, 3, 64, 2048], P('comp', 'tile'), may hold values from -6 to 6
- metric: float32 [4, 32, 2048], P('comp', 'tile'), may hold values from 0.5 to 2
- column_op: float32 [4, 64, 64], P('comp'), may hold values from -0.009375 to 1.0125
- links: int32 [4, 32, 6, 2048], P('comp', 'tile'), may hold values from -1 to 2303, as said below
- rims: int32 [4, 32, 2, 128], P('comp', 'tile'), may hold values from 0 to 2047
- out_map: int32 [4, 32, 32, 2, 128], P('comp', 'tile'), may hold values from -1 to 2047, as said below
- out_weight: float32 [4, 32, 32, 128], P('comp', 'tile'), may hold values from 0.25 to 1
- back_map: int32 [4, 32, 32, 2, 128], P('comp', 'tile'), may hold values from -1 to 2047, as said below
- back_weight: float32 [4, 32, 32, 128], P('comp', 'tile'), may hold values from 0.25 to 1
Outputs:
- new_state: float32 [4, 32, 3, 64, 2048], P('comp', 'tile')
The draws below stay inside these ranges and needn't reach their ends.
Inputs may be any that keep to these rules, and one draw needn't show every extreme that they name: -1 marks no link; others are positions in the extended block of 2304 entries. Atmosphere nodes have 3 links at element corners, 1 on element edges, none inside (rows 3 to 5 are -1); ocean cells have 6. `out_map`: source node and target cell are -1 together, exactly in the slots at or beyond a pair's count of rows; a pair carries at most 128 rows, and for each atmosphere group c some ocean tile receives 128 rows from every block of c; the ocean tiles' entries are all -1. `back_map`: source cell and target node are -1 together, exactly in the slots at or beyond a pair's count of rows; a pair carries at most 128 rows, and for each atmosphere group c some block of c receives 128 rows from every ocean tile; the ocean tiles' entries are all -1.
All inputs are finite; a program needn't handle non-finite values.
Results may differ from the reference program's by a relative error of at most 0.0003.
Values sent between devices are 32-bit elements; how exact they have to be, the bound alone decides.
No kernel may reach another device: no remote copies, remote signals or barrier semaphores. Data moves between devices by JAX's collectives and lax.ppermute only.
A program may use at most 256 MiB of HBM per device.

```python
import math
import jax
import jax.numpy as jnp
import numpy as np
from jax import lax

NODES = 2048
LEV = 64
FIELDS = 3
RIM = 128
SLOT = 128
N_COMP = 4
N_TILE = 32


def remap_table(key):
    keys = jax.random.split(key, 4)
    counts = jax.random.randint(keys[0], (N_COMP, N_TILE, N_TILE), 0, SLOT + 1)
    full_tile = jax.random.randint(keys[1], (N_COMP, 1, 1), 0, N_TILE)
    other = jnp.arange(N_TILE)[None, None, :]
    counts = jnp.where(other == full_tile, SLOT, counts)
    groups = jnp.arange(N_COMP)[:, None, None]
    counts = jnp.where(groups == N_COMP - 1, 0, counts)
    position = jnp.arange(SLOT)
    valid = position[None, None, None, :] < counts[..., None]
    sources = jax.random.randint(keys[2], (N_COMP, N_TILE, N_TILE, SLOT), 0, NODES)
    targets = jax.random.randint(keys[3], (N_COMP, N_TILE, N_TILE, SLOT), 0, NODES)
    at_full = (other == full_tile)[..., None]
    sources = jnp.where(at_full & (position == 0), NODES - 1, jnp.where(at_full & (position == 1), 0, sources))
    targets = jnp.where(at_full & (position == 0), NODES - 1, jnp.where(at_full & (position == 1), 0, targets))
    table = jnp.stack([sources, targets], axis=3)
    return jnp.where(valid[:, :, :, None, :], table, -1).astype(jnp.int32)


def draw_out_map(key, part):
    key = jax.random.fold_in(key, 21)
    return remap_table(key)


def draw_back_map(key, part):
    key = jax.random.fold_in(key, 37)
    return remap_table(key)


def draw_links(key, part):
    key = jax.random.fold_in(key, 11)
    keys = jax.random.split(key, 2)
    node = jnp.arange(NODES)
    local = node % 16
    row_pos = local // 4
    col_pos = local % 4
    edge_row = (row_pos == 0) | (row_pos == 3)
    edge_col = (col_pos == 0) | (col_pos == 3)
    partners = jnp.where(edge_row & edge_col, 3, jnp.where(edge_row | edge_col, 1, 0))
    shape = (N_COMP, N_TILE, 6, NODES)
    reach = jax.random.randint(keys[0], shape, 1, RIM + 1)
    side = jax.random.randint(keys[1], shape, 0, 2) * 2 - 1
    position = RIM + node[None, None, None, :] + reach * side
    which = jnp.arange(6)[:, None]
    groups = jnp.arange(N_COMP)[:, None, None, None]
    valid = jnp.where(groups == N_COMP - 1, True, (which < partners[None, :])[None, None])
    ocean = groups == N_COMP - 1
    position = jnp.where(ocean & (which == 0) & (node == NODES - 1), NODES + 2 * RIM - 1, position)
    position = jnp.where(ocean & (which == 1) & (node == 0), 0, position)
    return jnp.where(valid, position, -1).astype(jnp.int32)


def draw_rims(key, part):
    key = jax.random.fold_in(key, 13)
    offset = jax.random.randint(key, (N_COMP, N_TILE, 2, RIM), 0, 2 * RIM)
    side = jnp.arange(2)[:, None]
    entry = jnp.arange(RIM)[None, :]
    offset = jnp.where(entry == 0, 0, offset)
    chosen = jnp.where(side == 0, offset, NODES - 1 - offset)
    return chosen.astype(jnp.int32)


def draw_column_op(key, part):
    key = jax.random.fold_in(key, 5)
    extra = jax.random.uniform(key, (N_COMP, LEV, LEV), jnp.float32, -1.0, 1.0) * (0.6 / LEV)
    return (jnp.eye(LEV, dtype=jnp.float32)[None] + extra).astype(jnp.float32)


def levels(own_key, extent, pieces, smallest, high):
    loudness, own = 1.0, jax.random.fold_in(own_key, 6)
    for axis_at, parts in pieces:
        heights = jnp.exp(jax.random.uniform(jax.random.fold_in(own, axis_at), (parts,), jnp.float32, smallest / len(pieces), high / len(pieces)))
        loudness = loudness * jnp.repeat(heights, extent[axis_at] // parts).reshape([-1 if axis == axis_at else 1 for axis in range(len(extent))])
    return loudness


def gaussian(rng, dims, scale, limit, cuts=(), kind=jnp.bfloat16):
    entries = scale * jax.random.normal(rng, dims, jnp.float32)
    if cuts:
        entries = entries * levels(rng, dims, cuts, -0.22, 0.18)
    return jnp.clip(entries, -limit, limit).astype(kind)


def setup_inputs(seed: int = 0) -> dict:
    key_list = jax.random.split(jax.random.key(seed), 10)
    state = gaussian(key_list[0], (N_COMP, N_TILE, FIELDS, LEV, NODES), 1.0, 6.0, ((0, 4), (1, 32)), jnp.float32)
    metric = jnp.clip(jnp.exp(math.log(2.0) - 1.3862944 * jax.random.uniform(key_list[1], (N_COMP, N_TILE, NODES), jnp.float32) ** levels(key_list[1], (N_COMP, N_TILE, NODES), ((0, 4), (1, 32)), -0.2, 0.2)), 0.5, 2.0)
    column_op = draw_column_op(jax.random.fold_in(key_list[9], 71), 0)
    links = draw_links(jax.random.fold_in(key_list[9], 71), 0)
    rims = draw_rims(jax.random.fold_in(key_list[9], 71), 0)
    out_map = draw_out_map(jax.random.fold_in(key_list[9], 71), 0)
    out_weight = jnp.clip(jnp.exp(math.log(1.0) - 1.3862944 * jax.random.uniform(key_list[6], (N_COMP, N_TILE, N_TILE, SLOT), jnp.float32) ** levels(key_list[6], (N_COMP, N_TILE, N_TILE, SLOT), ((0, 4), (1, 32)), -0.2, 0.2)), 0.25, 1.0)
    back_map = draw_back_map(jax.random.fold_in(key_list[9], 71), 0)
    back_weight = jnp.clip(jnp.exp(math.log(1.0) - 1.3862944 * jax.random.uniform(key_list[8], (N_COMP, N_TILE, N_TILE, SLOT), jnp.float32) ** levels(key_list[8], (N_COMP, N_TILE, N_TILE, SLOT), ((0, 4), (1, 32)), -0.2, 0.2)), 0.25, 1.0)
    return dict(state=state, metric=metric, column_op=column_op, links=links, rims=rims, out_map=out_map, out_weight=out_weight, back_map=back_map, back_weight=back_weight)


VISCOSITY = 0.05
ATM_STEP = 0.02
OCEAN_RATE = 0.08
COUPLING = 0.5

def gll_blocks():
    points = np.array([-1.0, -1.0 / math.sqrt(5.0), 1.0 / math.sqrt(5.0), 1.0])
    legendre = 0.5 * (5.0 * points * points * points - 3.0 * points)
    matrix = np.zeros((4, 4))
    for first_point in range(4):
        for second_point in range(4):
            if first_point != second_point:
                matrix[first_point, second_point] = legendre[first_point] / (legendre[second_point] * (points[first_point] - points[second_point]))
    matrix[0, 0] = -3.0
    matrix[3, 3] = 3.0
    along_xi = np.kron(np.eye(4), matrix)
    along_eta = np.kron(matrix, np.eye(4))
    return (jnp.asarray(np.kron(np.eye(8), along_xi), dtype=jnp.float32), jnp.asarray(np.kron(np.eye(8), along_eta), dtype=jnp.float32))

def apply_block(values, block):
    shape = values.shape
    grouped = values.reshape(shape[:-1] + (shape[-1] // 128, 128))
    result = jnp.einsum('...m,nm->...n', grouped, block, precision=lax.Precision.HIGHEST)
    return result.reshape(shape)

def atmos_tendency(current, metric):
    block_xi, block_eta = gll_blocks()
    grad_xi = apply_block(current, block_xi)
    grad_eta = apply_block(current, block_eta)
    second = apply_block(grad_xi, block_xi) + apply_block(grad_eta, block_eta)
    wind_u = current[0][None]
    wind_v = current[1][None]
    return -metric * (wind_u * grad_xi + wind_v * grad_eta) + VISCOSITY * metric * metric * second

def pack_rows(values, sources, weight):
    picked = jnp.take(values, jnp.maximum(sources, 0), axis=1)
    return jnp.where(sources >= 0, picked, 0.0) * weight

def land_rows(rows, cells, count):
    target = jnp.where(cells >= 0, cells, count)
    summed = jax.ops.segment_sum(rows.T, target, num_segments=count + 1)
    return summed[:count].T

def linked_rows(extended, links):
    total = jnp.zeros(extended.shape[:2] + (links.shape[1],), jnp.float32)
    number = jnp.zeros((links.shape[1],), jnp.float32)
    for which in range(links.shape[0]):
        index = links[which]
        valid = index >= 0
        picked = jnp.take(extended, jnp.maximum(index, 0), axis=2)
        total = total + jnp.where(valid, picked, 0.0)
        number = number + valid.astype(jnp.float32)
    return (total, number)

def finish(updated, forcing, column):
    updated = updated.at[:, 0, :].add(COUPLING * forcing)
    return jnp.einsum('kl,fln->fkn', column, updated, precision=lax.Precision.HIGHEST)

def atmos_update(current, field, extended, links, metric, forcing, column):
    total, number = linked_rows(extended, links)
    updated = current + ATM_STEP * (field + total) / (1.0 + number)
    return finish(updated, forcing, column)

def ocean_update(current, field, extended, links, metric, forcing, column):
    total, number = linked_rows(extended, links)
    updated = current + OCEAN_RATE * metric * (total - number * current)
    return finish(updated, forcing, column)

def reference(state, metric, column_op, links, rims, out_map, out_weight, back_map, back_weight):
    ncomp = N_COMP
    ntile = N_TILE
    total_blocks = ncomp * ntile
    nodes = NODES
    comp_of = (jnp.arange(total_blocks) // ntile).astype(jnp.int32)

    def flat(array):
        return array.reshape((total_blocks,) + array.shape[2:])

    def first_pass(item):
        current, metric_one, comp_one = item
        return jnp.where(comp_one == ncomp - 1, current, atmos_tendency(current, metric_one))
    field = lax.map(first_pass, (flat(state), flat(metric), comp_of))

    def make_pack(field_one, rim_one):
        return jnp.concatenate([jnp.take(field_one, rim_one[0], axis=2), jnp.take(field_one, rim_one[1], axis=2)], axis=2)
    packs = jax.vmap(make_pack)(field, flat(rims))
    previous = jnp.roll(packs[..., RIM:], 1, axis=0)
    following = jnp.roll(packs[..., :RIM], -1, axis=0)
    block_index = jnp.arange(total_blocks)[:, None, None, None]
    boundary = (ncomp - 1) * ntile
    left = jnp.where((block_index == 0) | (block_index == boundary), 0.0, previous)
    right = jnp.where((block_index == total_blocks - 1) | (block_index == boundary - 1), 0.0, following)
    extended = jnp.concatenate([left, field, right], axis=-1)
    comp_grid = jnp.arange(ncomp)[:, None, None, None, None]
    surface = state[:, :, :, 0, :]
    packed_out = jax.vmap(jax.vmap(pack_rows))(surface, out_map[:, :, :, 0, :], out_weight)
    received = packed_out.transpose(0, 3, 2, 1, 4).reshape(ncomp, ntile, FIELDS, ntile * SLOT)
    cells = out_map[:, :, :, 1, :].transpose(0, 2, 1, 3).reshape(ncomp, ntile, ntile * SLOT)
    land_one = lambda rows, where_to: land_rows(rows, where_to, nodes)
    partial_value = jax.vmap(jax.vmap(land_one))(received, cells)
    partial_value = jnp.where(comp_grid[..., 0] == ncomp - 1, 0.0, partial_value)
    forcing_ocean = lax.optimization_barrier(jnp.sum(partial_value, axis=0))
    sea = surface[ncomp - 1]
    pack_back = jax.vmap(jax.vmap(pack_rows), in_axes=(None, 0, 0))
    packed_back = pack_back(sea, back_map[:, :, :, 0, :], back_weight)
    received_back = packed_back.transpose(0, 3, 2, 1, 4).reshape(ncomp, ntile, FIELDS, ntile * SLOT)
    cells_back = back_map[:, :, :, 1, :].transpose(0, 2, 1, 3).reshape(ncomp, ntile, ntile * SLOT)
    forcing_atmos = jax.vmap(jax.vmap(land_one))(received_back, cells_back)
    forcing = jnp.where(comp_grid[..., 0] == ncomp - 1, forcing_ocean[None], forcing_atmos)
    columns = column_op[comp_of]

    def second_pass(item):
        current, field_one, extended_one, links_one, metric_one, forcing_one, column_one, comp_one = item
        ocean_value = ocean_update(current, field_one, extended_one, links_one, metric_one, forcing_one, column_one)
        atmos_value = atmos_update(current, field_one, extended_one, links_one, metric_one, forcing_one, column_one)
        return jnp.where(comp_one == ncomp - 1, ocean_value, atmos_value)
    result = lax.map(second_pass, (flat(state), field, extended, flat(links), flat(metric), flat(forcing), columns, comp_of))
    return result.reshape(state.shape)
```

```python
import functools
import math

import jax
import jax.numpy as jnp
import numpy as np
from jax import lax
from jax.experimental import pallas as pl
from jax.experimental.pallas import tpu as pltpu
from jax.sharding import PartitionSpec as P

VISCOSITY = 0.05
ATM_STEP = 0.02
OCEAN_RATE = 0.08
COUPLING = 0.5
LANES = 128
BF = jnp.bfloat16
F32 = jnp.float32
VMEM_LIMIT = 48 * 1024 * 1024


def gll_matrix():
    points = np.array([-1.0, -1.0 / math.sqrt(5.0), 1.0 / math.sqrt(5.0), 1.0])
    legendre = 0.5 * (5.0 * points * points * points - 3.0 * points)
    matrix = np.zeros((4, 4))
    for a in range(4):
        for b in range(4):
            if a != b:
                matrix[a, b] = legendre[a] / (legendre[b] * (points[a] - points[b]))
    matrix[0, 0] = -3.0
    matrix[3, 3] = 3.0
    return matrix


def derivative_table():
    matrix = gll_matrix()
    along_xi = np.kron(np.eye(4), matrix)
    along_eta = np.kron(matrix, np.eye(4))
    second = along_xi @ along_xi + along_eta @ along_eta
    parts = [np.kron(np.eye(8), part).T for part in (along_xi, along_eta, second)]
    full = np.concatenate(parts, axis=1).astype(np.float32)
    high = full.astype(BF)
    low = (full - high.astype(np.float32)).astype(BF)
    return jnp.asarray(high), jnp.asarray(low)


def split(values):
    high = values.astype(BF)
    low = (values - high.astype(F32)).astype(BF)
    return high, low


def dot(a, b):
    return jnp.dot(a, b, preferred_element_type=F32)


def dot_nt(a, b):
    return lax.dot_general(a, b, (((1,), (1,)), ((), ())), preferred_element_type=F32)


def lane_pick(chunk_of, chunks, index):
    low = jnp.bitwise_and(index, LANES - 1)
    high = jnp.right_shift(index, 7)
    total = jnp.zeros(index.shape, F32)
    for at in range(chunks):
        row = jnp.broadcast_to(chunk_of(at), index.shape)
        picked = jnp.take_along_axis(row, low, axis=1, mode="promise_in_bounds")
        total = jnp.where(high == at, picked, total)
    return total


def out_kernel(flag, state, table, weight, payload):
    fields = state.shape[0]
    chunks = state.shape[2] // LANES

    @pl.when(flag[0] == 0)
    def _():
        source = table[:, 0, :]
        scale = weight[...]
        for f in range(fields):
            rows = lane_pick(lambda at: state[f, 0:1, at * LANES : (at + 1) * LANES], chunks, source)
            payload[:, f, :] = rows * scale
        payload[:, fields, :] = table[:, 1, :].astype(F32)

    @pl.when(flag[0] == 1)
    def _():
        payload[...] = jnp.zeros(payload.shape, F32)
        for f in range(fields):
            for at in range(chunks):
                payload[at, f : f + 1, :] = state[f, 0:1, at * LANES : (at + 1) * LANES]


def back_kernel(flag, got0, got1, got2, table, weight, payload):
    fields = got0.shape[1] - 1
    chunks = 16
    wide = fields + 1

    @pl.when(flag[0] == 0)
    def _():
        source = table[:, 0, :]
        scale = weight[...]
        for f in range(fields):
            pick = lambda at: got0[at, f : f + 1, :] + got1[at, f : f + 1, :] + got2[at, f : f + 1, :]
            rows = lane_pick(pick, chunks, source)
            payload[:, f, :] = rows * scale
        payload[:, fields, :] = table[:, 1, :].astype(F32)
        payload[:, wide:, :] = jnp.zeros((payload.shape[0], payload.shape[1] - wide, LANES), F32)

    @pl.when(flag[0] == 1)
    def _():
        payload[:, 0:wide, :] = got0[...]
        payload[:, wide : 2 * wide, :] = got1[...]
        payload[:, 2 * wide : 3 * wide, :] = got2[...]


def field_kernel(flag, state, metric, table_high, table_low, rims, high_ref, low_ref, left_ref, right_ref):
    rows, nodes = high_ref.shape
    third = rows // 3

    @pl.when(flag[0] == 0)
    def _():
        def chunk(at, carry):
            where = pl.ds(pl.multiple_of(at * LANES, LANES), LANES)
            values = state[:, where]
            high, low = split(values)
            both = dot(jnp.concatenate([high, low], axis=0), table_high[...])
            grads = both[:rows] + both[rows:] + dot(high, table_low[...])
            grad_xi = grads[:, :LANES]
            grad_eta = grads[:, LANES : 2 * LANES]
            second = grads[:, 2 * LANES :]
            scale = metric[0:1, where]
            wind_u = values[:third]
            wind_v = values[third : 2 * third]
            wind_u = jnp.concatenate([wind_u] * 3, axis=0)
            wind_v = jnp.concatenate([wind_v] * 3, axis=0)
            field = -scale * (wind_u * grad_xi + wind_v * grad_eta) + (VISCOSITY * scale * scale) * second
            fh, fl = split(field)
            high_ref[:, where] = fh
            low_ref[:, where] = fl
            return carry

        lax.fori_loop(0, nodes // LANES, chunk, 0)

    @pl.when(flag[0] == 1)
    def _():
        high, low = split(state[...])
        high_ref[...] = high
        low_ref[...] = low

    ids = lax.broadcasted_iota(jnp.int32, (nodes, LANES), 0)
    for side, target in ((0, left_ref), (1, right_ref)):
        onehot = jnp.where(ids == rims[side : side + 1, :], 1.0, 0.0).astype(BF)
        target[...] = dot(high_ref[...], onehot) + dot(low_ref[...], onehot)


def link_kernel(flag, high, low, left, right, state, metric, links, column, mixed, ext, count):
    rows, nodes = state.shape
    levels = column.shape[0]
    rim = left.shape[1]
    width = 2 * LANES
    blocks = (nodes + 2 * rim) // LANES
    lh, ll = split(left[...])
    rh, rl = split(right[...])
    ext[0:rows, 0:rim] = lh
    ext[rows:, 0:rim] = ll
    ext[0:rows, rim : rim + nodes] = high[...]
    ext[rows:, rim : rim + nodes] = low[...]
    ext[0:rows, rim + nodes :] = rh
    ext[rows:, rim + nodes :] = rl
    col_high, col_low = split(column[...])
    col = jnp.concatenate([col_high, col_low], axis=0)

    def run(rows_used, ocean):
        def tile(at, carry):
            where = pl.ds(pl.multiple_of(at * width, width), width)
            index = links[:, where]
            number = jnp.sum((index >= 0).astype(F32), axis=0, keepdims=True)
            lane_low = jnp.bitwise_and(index, LANES - 1)
            lane_high = jnp.right_shift(index, 7)
            ids = lax.broadcasted_iota(jnp.int32, (LANES, width), 0)
            lows = []
            highs = []
            for k in range(rows_used):
                lows.append(jnp.where(ids == lane_low[k : k + 1, :], 1.0, 0.0).astype(BF).reshape(8, 16, width))
                highs.append(jnp.broadcast_to(lane_high[k : k + 1, :], (16, width)).astype(BF))
            for block in range(blocks):
                total = None
                for k in range(rows_used):
                    mask = jnp.where(highs[k] == block, 1.0, 0.0).astype(BF)
                    term = lows[k] * mask[None]
                    total = term if total is None else total + term
                count[block * LANES : (block + 1) * LANES, :] = total.reshape(LANES, width)
            both = dot(ext[...], count[...])
            linked = both[:rows] + both[rows:]
            current = state[:, where]
            if ocean:
                gain = OCEAN_RATE * metric[0:1, where]
                updated = current + gain * (linked - number * current)
            else:
                gain = ATM_STEP / (1.0 + number)
                field = ext[0:rows, pl.ds(pl.multiple_of(at * width + rim, LANES), width)].astype(F32)
                field = field + ext[rows:, pl.ds(pl.multiple_of(at * width + rim, LANES), width)].astype(F32)
                updated = current + gain * (field + linked)
            uh, ul = split(updated)
            for f in range(rows // levels):
                part = slice(f * levels, (f + 1) * levels)
                full = dot(col, uh[part])
                mixed[part, where] = full[:levels] + full[levels:] + dot(col_high, ul[part])
            return carry

        lax.fori_loop(0, nodes // width, tile, 0)

    @pl.when(flag[0] == 0)
    def _():
        run(3, False)

    @pl.when(flag[0] == 1)
    def _():
        run(6, True)


def land_kernel(flag, got, mixed, column, result, left_rows, onehots):
    senders = got.shape[0]
    levels = column.shape[0]
    fields = 3
    chunks = 16
    ids = lax.broadcasted_iota(jnp.int32, (LANES, LANES), 0)
    ids_high = lax.broadcasted_iota(jnp.int32, (chunks, LANES), 0)

    def land(part, total):
        for a in range(senders):
            base = 4 * part
            cell = got[a, pl.ds(base + fields, 1), :].astype(jnp.int32)
            lane_low = jnp.bitwise_and(cell, LANES - 1)
            lane_high = jnp.right_shift(cell, 7)
            where = slice(a * LANES, (a + 1) * LANES)
            onehots[:, where] = jnp.where(ids == lane_low, 1.0, 0.0).astype(BF)
            mask = ids_high == lane_high
            picked = [jnp.where(mask, got[a, pl.ds(base + f, 1), :], 0.0) for f in range(fields)]
            high, low = split(jnp.concatenate(picked, axis=0))
            left_rows[0 : fields * chunks, where] = high
            left_rows[fields * chunks :, where] = low
        return total + dot_nt(left_rows[...], onehots[...])

    parts = jnp.where(flag[0] == 1, 3, 1)
    landed = lax.fori_loop(0, parts, land, jnp.zeros((2 * fields * chunks, LANES), F32))
    forcing = landed[: fields * chunks] + landed[fields * chunks :]
    gain = COUPLING * jnp.broadcast_to(column[:, 0:1], (levels, LANES))
    for f in range(fields):
        part = slice(f * levels, (f + 1) * levels)
        for at in range(chunks):
            where = slice(at * LANES, (at + 1) * LANES)
            result[part, where] = mixed[part, where] + gain * forcing[f * chunks + at : f * chunks + at + 1, :]


def call(kernel, flag, args, outs, scratch=(), specs=None):
    vmem = pl.BlockSpec(memory_space=pltpu.VMEM)
    specs = specs or [vmem] * len(args)
    return pl.pallas_call(
        kernel,
        in_specs=[pl.BlockSpec(memory_space=pltpu.SMEM)] + specs,
        out_specs=[vmem] * len(outs),
        out_shape=outs,
        scratch_shapes=list(scratch),
        compiler_params=pltpu.CompilerParams(vmem_limit_bytes=VMEM_LIMIT),
    )(flag, *args)


def per_device(state, metric, column_op, links, rims, out_map, out_weight, back_map, back_weight):
    _, _, fields, levels, nodes = state.shape
    rows = fields * levels
    rim = rims.shape[-1]
    ntile = lax.axis_size("tile")
    ncomp = lax.axis_size("comp")
    slot = out_map.shape[-1]
    both = ("comp", "tile")
    ocean_at = ncomp - 1
    total = ncomp * ntile
    edge = ocean_at * ntile - 1
    flag = (lax.axis_index("comp") == ocean_at).astype(jnp.int32).reshape(1)
    current = state.reshape(rows, nodes)
    metric_row = metric.reshape(1, nodes)
    column = column_op.reshape(levels, levels)
    vmem = pl.BlockSpec(memory_space=pltpu.VMEM)

    packed = jax.ShapeDtypeStruct((ntile, fields + 1, slot), F32)
    (payload,) = pl.pallas_call(
        out_kernel,
        grid=(1,),
        in_specs=[
            pl.BlockSpec(memory_space=pltpu.SMEM),
            pl.BlockSpec((fields, 8, nodes), lambda i: (0, 0, 0)),
            pl.BlockSpec((ntile, 2, slot), lambda i: (0, 0, 0)),
            pl.BlockSpec((ntile, slot), lambda i: (0, 0)),
        ],
        out_specs=[pl.BlockSpec((ntile, fields + 1, slot), lambda i: (0, 0, 0))],
        out_shape=[packed],
    )(flag, state.reshape(fields, levels, nodes), out_map.reshape(ntile, 2, slot), out_weight.reshape(ntile, slot))
    swapped = []
    for c in range(ocean_at):
        pairs = [(c * ntile + t, ocean_at * ntile + t) for t in range(ntile)]
        swapped.append(lax.ppermute(payload, both, pairs + [(b, a) for a, b in pairs]))

    table_high, table_low = derivative_table()
    half = jax.ShapeDtypeStruct((rows, nodes), BF)
    side = jax.ShapeDtypeStruct((rows, rim), F32)
    high, low, to_left, to_right = call(
        field_kernel,
        flag,
        (current, metric_row, table_high, table_low, rims.reshape(2, rim)),
        [half, half, side, side],
    )
    steps = [(i, i + 1) for i in range(total - 1) if i != edge]
    left = lax.ppermute(to_right, both, steps)
    right = lax.ppermute(to_left, both, [(b, a) for a, b in steps])

    (rows_out,) = call(
        back_kernel,
        flag,
        (*swapped, back_map.reshape(ntile, 2, slot), back_weight.reshape(ntile, slot)),
        [jax.ShapeDtypeStruct((ntile, ocean_at * (fields + 1), slot), F32)],
    )
    got = lax.all_to_all(rows_out, "tile", split_axis=0, concat_axis=0, tiled=True)

    full = jax.ShapeDtypeStruct((rows, nodes), F32)
    (mixed,) = call(
        link_kernel,
        flag,
        (high, low, left, right, current, metric_row, links.reshape(6, nodes), column),
        [full],
        [pltpu.VMEM((2 * rows, nodes + 2 * rim), BF), pltpu.VMEM((nodes + 2 * rim, 2 * LANES), BF)],
    )
    (result,) = call(
        land_kernel,
        flag,
        (got, mixed, column),
        [full],
        [pltpu.VMEM((2 * fields * (nodes // LANES), ntile * slot), BF), pltpu.VMEM((LANES, ntile * slot), BF)],
    )
    return result.reshape(state.shape)


def solution(mesh):
    return jax.shard_map(
        per_device,
        mesh=mesh,
        in_specs=(
            P("comp", "tile", None, None, None),
            P("comp", "tile", None),
            P("comp", None, None),
            P("comp", "tile", None, None),
            P("comp", "tile", None, None),
            P("comp", "tile", None, None, None),
            P("comp", "tile", None, None),
            P("comp", "tile", None, None, None),
            P("comp", "tile", None, None),
        ),
        out_specs=P("comp", "tile", None, None, None),
        check_vma=False,
    )
```

```python
import math

import jax
import jax.numpy as jnp
import numpy as np
from jax import lax
from jax.experimental import pallas as pl
from jax.experimental.pallas import tpu as pltpu
from jax.sharding import PartitionSpec as P

VISCOSITY = 0.05
ATM_STEP = 0.02
OCEAN_RATE = 0.08
COUPLING = 0.5
LANES = 128
BF = jnp.bfloat16
F32 = jnp.float32
MIB = 1024 * 1024
FINAL_LIMIT = 56


def gll_matrix():
    points = np.array([-1.0, -1.0 / math.sqrt(5.0), 1.0 / math.sqrt(5.0), 1.0])
    legendre = 0.5 * (5.0 * points * points * points - 3.0 * points)
    matrix = np.zeros((4, 4))
    for a in range(4):
        for b in range(4):
            if a != b:
                matrix[a, b] = legendre[a] / (legendre[b] * (points[a] - points[b]))
    matrix[0, 0] = -3.0
    matrix[3, 3] = 3.0
    return matrix


def derivative_table():
    matrix = gll_matrix()
    along_xi = np.kron(np.eye(4), matrix)
    along_eta = np.kron(matrix, np.eye(4))
    second = along_xi @ along_xi + along_eta @ along_eta
    parts = [np.kron(np.eye(8), part).T for part in (along_xi, along_eta, second)]
    full = np.concatenate(parts, axis=1).astype(np.float32)
    high = full.astype(BF)
    low = (full - high.astype(np.float32)).astype(BF)
    return jnp.asarray(np.concatenate([high, low], axis=0))


def split(values):
    high = values.astype(BF)
    low = (values - high.astype(F32)).astype(BF)
    return high, low


def dot(a, b):
    return jnp.dot(a, b, preferred_element_type=F32)


def dot_nt(a, b):
    return lax.dot_general(a, b, (((1,), (1,)), ((), ())), preferred_element_type=F32)


def lane_pick(chunk_of, chunks, index):
    low = jnp.bitwise_and(index, LANES - 1)
    high = jnp.right_shift(index, 7)
    total = jnp.zeros(index.shape, F32)
    for at in range(chunks):
        row = jnp.broadcast_to(chunk_of(at), index.shape)
        picked = jnp.take_along_axis(row, low, axis=1, mode="promise_in_bounds")
        total = jnp.where(high == at, picked, total)
    return total


def out_kernel(surface, table, weight, payload):
    atmos = lax.axis_index("comp") != lax.axis_size("comp") - 1
    fields = surface.shape[0]
    chunks = surface.shape[2] // LANES

    @pl.when(atmos)
    def _():
        source = table[:, 0, :]
        for f in range(fields):
            rows_of = lambda at: surface[f, 0:1, at * LANES : (at + 1) * LANES]
            payload[:, f, :] = lane_pick(rows_of, chunks, source) * weight[...]
        payload[:, fields, :] = table[:, 1, :].astype(F32)

    @pl.when(jnp.logical_not(atmos))
    def _():
        payload[...] = jnp.zeros(payload.shape, F32)
        for f in range(fields):
            for at in range(chunks):
                payload[at, f : f + 1, :] = surface[f, 0:1, at * LANES : (at + 1) * LANES]


def back_kernel(got0, got1, got2, table, weight, after, payload):
    comp = lax.axis_index("comp")
    fields = got0.shape[1] - 1
    chunks = 16
    wide = fields + 1

    @pl.when(comp != 3)
    def _():
        source = table[:, 0, :]
        scale = weight[...]
        for f in range(fields):

            def pick(at):
                first, second, third = (got[at, f : f + 1, :] for got in (got0, got1, got2))
                return jnp.where(comp == 0, first, jnp.where(comp == 1, second, third))

            rows = lane_pick(pick, chunks, source)
            payload[:, f, :] = rows * scale
        payload[:, fields, :] = table[:, 1, :].astype(F32)
        payload[:, wide:, :] = jnp.zeros((payload.shape[0], payload.shape[1] - wide, LANES), F32)

    @pl.when(comp == 3)
    def _():
        payload[:, 0:wide, :] = got0[...]
        payload[:, wide : 2 * wide, :] = got1[...]
        payload[:, 2 * wide : 3 * wide, :] = got2[...]


def pick_rims(wanted, parts):
    nodes = parts.shape[1]
    rows = parts.shape[0] // 2
    ids = lax.broadcasted_iota(jnp.int16, (nodes, LANES), 0)
    wanted = jnp.broadcast_to(wanted, (16, LANES)).astype(jnp.int16)
    wanted = jnp.broadcast_to(wanted[None], (nodes // 16, 16, LANES)).reshape(nodes, LANES)
    onehot = jnp.where(ids == wanted, jnp.ones((), BF), jnp.zeros((), BF))
    both = dot(parts[...], onehot)
    return both[:rows] + both[rows:]


def count_links(index, order, target):
    width = target.shape[1]
    one = jnp.ones((16, width), BF)
    zero = jnp.zeros((16, width), BF)
    ids = lax.broadcasted_iota(jnp.int16, (16, width), 0)
    low_off = [
        jnp.broadcast_to(jnp.bitwise_and(row, LANES - 1), (16, width)).astype(jnp.int16) - ids for row in index
    ]
    highs = [jnp.broadcast_to(jnp.right_shift(row, 7), (16, width)).astype(BF) for row in index]
    masks = [[jnp.where(high == block, one, zero) for high in highs] for block in order]
    for sub in range(LANES // 16):
        lows = [jnp.where(off == sub * 16, one, zero) for off in low_off]
        for slot in range(len(order)):
            total = None
            for low, mask in zip(lows, masks[slot]):
                term = low * mask
                total = term if total is None else total + term
            target[slot * LANES + sub * 16 : slot * LANES + sub * 16 + 16, :] = total

def gain_of(ocean, number, metric):
    return OCEAN_RATE * metric if ocean else ATM_STEP / (1.0 + number)

def atmos_field(values, scale, table_high, table_low):
    third = values.shape[0] // 3
    high, low = split(values)
    grads = dot(high, table_high) + dot(low, table_high) + dot(high, table_low)
    grad_xi = grads[:, :LANES]
    grad_eta = grads[:, LANES : 2 * LANES]
    second = grads[:, 2 * LANES :]
    wind_u = jnp.concatenate([values[:third]] * 3, axis=0)
    wind_v = jnp.concatenate([values[third : 2 * third]] * 3, axis=0)
    return (VISCOSITY * scale * scale) * second - scale * (wind_u * grad_xi + wind_v * grad_eta)


def field_kernel(state, metric, tables, rims, after, parts, left_ref, right_ref):
    atmos = lax.axis_index("comp") != lax.axis_size("comp") - 1
    rows, nodes = state.shape

    @pl.when(atmos)
    def _():
        for at in range(nodes // LANES):
            where = slice(at * LANES, (at + 1) * LANES)
            field = atmos_field(state[:, where], metric[0:1, where], tables[:LANES, :], tables[LANES:, :])
            high, low = split(field)
            parts[0:rows, where] = high
            parts[rows:, where] = low

    @pl.when(jnp.logical_not(atmos))
    def _():
        high, low = split(state[...])
        parts[0:rows, :] = high
        parts[rows:, :] = low

    left_ref[...] = pick_rims(rims[0:1, :], parts)
    right_ref[...] = pick_rims(rims[1:2, :], parts)


def inner_kernel(parts, state, metric, links, after, partial, count):
    atmos = lax.axis_index("comp") != lax.axis_size("comp") - 1
    rows, nodes = state.shape
    unroll, _, width = count.shape
    chunks = nodes // LANES
    def run(used, is_ocean):
        def step(at, here):
            where = pl.ds(pl.multiple_of(at * width, width), width)
            index = [links[k, :, where] for k in range(used)]
            number = sum((row >= 0).astype(F32) for row in index)
            count_links(index, list(range(1, chunks + 1)), here)
            both = dot(parts[...], here[...])
            linked = both[:rows] + both[rows:]
            current = state[:, where]
            gain = gain_of(is_ocean, number, metric[0:1, where])
            if is_ocean:
                partial[:, where] = current + gain * (linked - number * current)
            else:
                field = parts[0:rows, where].astype(F32) + parts[rows:, where].astype(F32)
                partial[:, where] = current + gain * (field + linked)

        def group(i, carry):
            for u in range(unroll):
                step(i * unroll + u, count.at[u])
            return carry

        lax.fori_loop(0, nodes // width // unroll, group, 0)

    @pl.when(atmos)
    def _():
        run(3, False)

    @pl.when(jnp.logical_not(atmos))
    def _():
        run(6, True)


def count_links(index, order, target):
    width = target.shape[1]
    one = jnp.ones((16, width), BF)
    zero = jnp.zeros((16, width), BF)
    ids = lax.broadcasted_iota(jnp.int16, (16, width), 0)
    low_off = [
        jnp.broadcast_to(jnp.bitwise_and(row, LANES - 1), (16, width)).astype(jnp.int16) - ids for row in index
    ]
    highs = [jnp.broadcast_to(jnp.right_shift(row, 7), (16, width)).astype(BF) for row in index]
    masks = [[jnp.where(high == block, one, zero) for high in highs] for block in order]
    for sub in range(LANES // 16):
        lows = [jnp.where(off == sub * 16, one, zero) for off in low_off]
        for slot in range(len(order)):
            total = None
            for low, mask in zip(lows, masks[slot]):
                term = low * mask
                total = term if total is None else total + term
            target[slot * LANES + sub * 16 : slot * LANES + sub * 16 + 16, :] = total

def gain_of(ocean, number, metric):
    return OCEAN_RATE * metric if ocean else ATM_STEP / (1.0 + number)

def rims_there(left, right, token):
    token[...] = jnp.zeros(token.shape, F32)


def final_kernel(
    partial_in, left_in, right_in, got_in, metric_in, links_in, column_in, after, result,
    partial, sides, got, metric, links, column, done, rim_parts, count, left_rows, onehots, sems,
):
    comp = lax.axis_index("comp")
    tile = lax.axis_index("tile")
    last_comp = lax.axis_size("comp") - 1
    last_tile = lax.axis_size("tile") - 1
    ocean = comp == last_comp
    atmos = jnp.logical_not(ocean)
    has_left = jnp.logical_not((tile == 0) & (ocean | (comp == 0)))
    has_right = jnp.logical_not((tile == last_tile) & (comp >= last_comp - 1))
    rows, nodes = partial.shape
    levels = column.shape[0]
    senders = got.shape[0]
    rim = left_in.shape[1]
    unroll, _, width = count.shape
    tiles = nodes // width
    fields = rows // levels
    chunks = nodes // LANES
    columns = [pl.ds(n * width, width) for n in range(tiles)]
    moves = [(got_in, got), (links_in, links), (left_in, sides.at[0]), (right_in, sides.at[1])]
    moves += [(metric_in, metric), (column_in, column)]
    moves += [(partial_in.at[:, where], partial.at[:, where]) for where in columns]
    copies = [pltpu.make_async_copy(a, b, sems.at[n]) for n, (a, b) in enumerate(moves)]
    for copy in copies:
        copy.start()
    copies[0].wait()
    ids = lax.broadcasted_iota(jnp.int32, (LANES, LANES), 0)
    ids_high = lax.broadcasted_iota(jnp.int32, (chunks, LANES), 0)

    def land(part, total):
        for a in range(senders):
            base = 4 * part
            cell = got[a, pl.ds(base + fields, 1), :].astype(jnp.int32)
            lane_low = jnp.bitwise_and(cell, LANES - 1)
            lane_high = jnp.right_shift(cell, 7)
            where = slice(a * LANES, (a + 1) * LANES)
            onehots[:, where] = jnp.where(ids == lane_low, 1.0, 0.0).astype(BF)
            mask = ids_high == lane_high
            picked = [jnp.where(mask, got[a, pl.ds(base + f, 1), :], 0.0) for f in range(fields)]
            high, low = split(jnp.concatenate(picked, axis=0))
            left_rows[0 : fields * chunks, where] = high
            left_rows[fields * chunks :, where] = low
        return total + dot_nt(left_rows[...], onehots[...])

    groups = jnp.where(ocean, last_comp, 1)
    landed = lax.fori_loop(0, groups, land, jnp.zeros((2 * fields * chunks, LANES), F32))
    forcing = COUPLING * (landed[: fields * chunks] + landed[fields * chunks :])

    for copy in copies[1:6]:
        copy.wait()
    for side, there in ((0, has_left), (1, has_right)):
        high, low = split(jnp.where(there, sides[side], 0.0))
        rim_parts[0:rows, side * rim : (side + 1) * rim] = high
        rim_parts[rows:, side * rim : (side + 1) * rim] = low
    col_high, col_low = split(column[...])
    col_gain = column[:, 0:1]
    col = jnp.concatenate([col_high, col_low], axis=0)

    def move(at):
        return pltpu.make_async_copy(done.at[:, columns[at]], result.at[:, columns[at]], sems.at[6 + tiles + at])

    def run(used, is_ocean):
        for at in range(tiles):
            where = slice(at * width, (at + 1) * width)
            here = count.at[at % unroll]
            index = [links[k, :, where] for k in range(used)]
            number = sum((row >= 0).astype(F32) for row in index)
            count_links(index, [0, chunks + 1], here)
            both = dot(rim_parts[...], here[...])
            gain = gain_of(is_ocean, number, metric[0:1, where])
            copies[6 + at].wait()
            updated = partial[:, where] + gain * (both[:rows] + both[rows:])
            uh, ul = split(updated)
            for f in range(fields):
                part = slice(f * levels, (f + 1) * levels)
                full = dot(col, uh[part])
                mixed = full[:levels] + full[levels:] + dot(col_high, ul[part])
                first = f * chunks + at * width // LANES
                rows_of = [forcing[n : n + 1, :] for n in range(first, first + width // LANES)]
                done[part, where] = mixed + col_gain * jnp.concatenate(rows_of, axis=1)
            move(at).start()

    @pl.when(atmos)
    def _():
        run(3, False)

    @pl.when(ocean)
    def _():
        run(6, True)

    for at in range(tiles):
        move(at).wait()


def call(kernel, args, outs, scratch=(), limit=32, form="vmem", anywhere=(), cost=None):
    free = pl.BlockSpec(memory_space=pl.ANY)
    whole = pl.BlockSpec(memory_space=pltpu.VMEM)

    def spec(dims):
        if form == "block":
            return pl.BlockSpec(dims, lambda i: (0,) * len(dims))
        return free if form == "any" else whole

    params = pltpu.CompilerParams() if limit is None else pltpu.CompilerParams(vmem_limit_bytes=limit * MIB)
    return pl.pallas_call(
        kernel,
        grid=(1,) if form == "block" else (),
        in_specs=[free if n in anywhere else spec(arg.shape) for n, arg in enumerate(args)],
        out_specs=[spec(out.shape) for out in outs],
        out_shape=outs,
        scratch_shapes=list(scratch),
        compiler_params=params,
        cost_estimate=cost and pl.CostEstimate(flops=cost, bytes_accessed=4_000_000, transcendentals=0),
    )(*args)


def per_device(state, metric, column_op, links, rims, out_map, out_weight, back_map, back_weight):
    _, _, fields, levels, nodes = state.shape
    rows = fields * levels
    rim = rims.shape[-1]
    ntile = lax.axis_size("tile")
    ncomp = lax.axis_size("comp")
    slot = out_map.shape[-1]
    axes = ("comp", "tile")
    total = ncomp * ntile
    chunks = nodes // LANES
    width = 2 * LANES
    tiles = nodes // width
    metric_row = metric.reshape(1, nodes)
    link_rows = links.reshape(6, 1, nodes)
    tables = derivative_table()
    dma = pltpu.SemaphoreType.DMA
    int32 = jnp.int32

    def shape(*dims, kind=F32):
        return jax.ShapeDtypeStruct(dims, kind)

    def held(*dims, kind=F32):
        return pltpu.VMEM(dims, kind)

    (payload,) = pl.pallas_call(
        out_kernel,
        grid=(1,),
        in_specs=[
            pl.BlockSpec((fields, 8, nodes), lambda i: (0, 0, 0)),
            pl.BlockSpec((ntile, 2, slot), lambda i: (0, 0, 0)),
            pl.BlockSpec((ntile, slot), lambda i: (0, 0)),
        ],
        out_specs=[pl.BlockSpec((ntile, fields + 1, slot), lambda i: (0, 0, 0))],
        out_shape=[shape(ntile, fields + 1, slot)],
    )(state.reshape(fields, levels, nodes), out_map.reshape(ntile, 2, slot), out_weight.reshape(ntile, slot))

    def across(values, flip):
        pairs = [(a * ntile + b, (a ^ flip) * ntile + b) for a in range(ncomp) for b in range(ntile)]
        return lax.ppermute(values, axes, pairs)

    got1 = across(payload, 2)
    got2 = across(payload, 1)
    got0 = across(got1, 1)

    current = state.reshape(rows, nodes)
    parts, to_left, to_right = call(
        field_kernel,
        (current, metric_row, tables, rims.reshape(2, rim), payload),
        [shape(2 * rows, nodes, kind=BF), shape(rows, rim), shape(rows, rim)],
        anywhere=(4,),
        cost=4_000_000_000,
    )
    steps = [(i, (i + 1) % total) for i in range(total)]
    left = lax.ppermute(to_right, axes, steps)
    right = lax.ppermute(to_left, axes, [(b, a) for a, b in steps])
    (rows_out,) = call(
        back_kernel,
        (got0, got1, got2, back_map.reshape(ntile, 2, slot), back_weight.reshape(ntile, slot), to_left),
        [shape(ntile, (ncomp - 1) * (fields + 1), slot)],
        anywhere=(5,),
    )
    got = lax.all_to_all(rows_out, "tile", split_axis=0, concat_axis=0, tiled=True)

    (partial,) = call(
        inner_kernel,
        (parts, current, metric_row, link_rows, rows_out),
        [shape(rows, nodes)],
        [held(2, nodes, width, kind=BF)],
        anywhere=(4,),
        cost=8_000_000_000,
    )

    (rims_token,) = call(rims_there, (left, right), [shape(8, LANES)], anywhere=(0, 1), cost=8_000_000_000)
    (result,) = call(
        final_kernel,
        (partial, left, right, got, metric_row, link_rows, column_op.reshape(levels, levels), rims_token),
        [shape(rows, nodes)],
        [
            held(rows, nodes),
            held(2, rows, rim),
            held(ntile, (ncomp - 1) * (fields + 1), slot),
            held(1, nodes),
            held(6, 1, nodes, kind=int32),
            held(levels, levels),
            held(rows, nodes),
            held(2 * rows, 2 * rim, kind=BF),
            held(2, 2 * rim, width, kind=BF),
            held(2 * fields * chunks, ntile * slot, kind=BF),
            held(LANES, ntile * slot, kind=BF),
            dma((6 + 2 * tiles,)),
        ],
        limit=FINAL_LIMIT,
        form="any",
    )
    return result.reshape(state.shape)


def solution(mesh):
    return jax.shard_map(
        per_device,
        mesh=mesh,
        in_specs=(
            P("comp", "tile", None, None, None),
            P("comp", "tile", None),
            P("comp", None, None),
            P("comp", "tile", None, None),
            P("comp", "tile", None, None),
            P("comp", "tile", None, None, None),
            P("comp", "tile", None, None),
            P("comp", "tile", None, None, None),
            P("comp", "tile", None, None),
        ),
        out_specs=P("comp", "tile", None, None, None),
        check_vma=False,
    )
```

```python
import math

import jax
import jax.numpy as jnp
import numpy as np
from jax import lax
from jax.experimental import pallas as pl
from jax.experimental.pallas import tpu as pltpu
from jax.sharding import PartitionSpec as P

VISCOSITY = 0.05
ATM_STEP = 0.02
OCEAN_RATE = 0.08
COUPLING = 0.5
LANES = 128
BF = jnp.bfloat16
F32 = jnp.float32
MIB = 1024 * 1024
HOLD = 5


def gll_matrix():
    points = np.array([-1.0, -1.0 / math.sqrt(5.0), 1.0 / math.sqrt(5.0), 1.0])
    legendre = 0.5 * (5.0 * points * points * points - 3.0 * points)
    matrix = np.zeros((4, 4))
    for a in range(4):
        for b in range(4):
            if a != b:
                matrix[a, b] = legendre[a] / (legendre[b] * (points[a] - points[b]))
    matrix[0, 0] = -3.0
    matrix[3, 3] = 3.0
    return matrix


def derivative_table():
    first = gll_matrix()
    twice = first @ first
    m = lax.broadcasted_iota(jnp.int32, (LANES, LANES), 0)
    n = lax.broadcasted_iota(jnp.int32, (LANES, LANES), 1)

    def entries(a, b, matrices):
        at = jnp.bitwise_and(a, 3) * 4 + jnp.bitwise_and(b, 3)
        values = [jnp.zeros((LANES, LANES), F32) for _ in matrices]
        for row in range(4):
            for column in range(4):
                hit = at == column * 4 + row
                values = [jnp.where(hit, float(p[row, column]), v) for p, v in zip(matrices, values)]
        return values

    same_row = jnp.right_shift(m, 2) == jnp.right_shift(n, 2)
    same_element = jnp.right_shift(m, 4) == jnp.right_shift(n, 4)
    same_column = same_element & (jnp.bitwise_and(m, 3) == jnp.bitwise_and(n, 3))
    xi, xi_twice = entries(m, n, (first, twice))
    eta, eta_twice = entries(jnp.right_shift(m, 2), jnp.right_shift(n, 2), (first, twice))
    parts = [
        jnp.where(same_row, xi, 0.0),
        jnp.where(same_column, eta, 0.0),
        jnp.where(same_row, xi_twice, 0.0) + jnp.where(same_column, eta_twice, 0.0),
    ]
    return split(jnp.concatenate(parts, axis=1))


def split(values):
    high = values.astype(BF)
    low = (values - high.astype(F32)).astype(BF)
    return high, low


def dot(a, b):
    return jnp.dot(a, b, preferred_element_type=F32)


def dot_nt(a, b):
    return lax.dot_general(a, b, (((1,), (1,)), ((), ())), preferred_element_type=F32)


def lane_pick(chunk_of, chunks, index):
    low = jnp.bitwise_and(index, LANES - 1)
    high = jnp.right_shift(index, 7)
    total = jnp.zeros(index.shape, F32)
    for at in range(chunks):
        row = jnp.broadcast_to(chunk_of(at), index.shape)
        picked = jnp.take_along_axis(row, low, axis=1, mode="promise_in_bounds")
        total = jnp.where(high == at, picked, total)
    return total


def out_kernel(surface, table, weight, payload):
    atmos = lax.axis_index("comp") != lax.axis_size("comp") - 1
    fields = surface.shape[0]
    chunks = surface.shape[2] // LANES

    @pl.when(atmos)
    def _():
        source = table[:, 0, :]
        for f in range(fields):
            rows_of = lambda at: surface[f, 0:1, at * LANES : (at + 1) * LANES]
            payload[:, f, :] = lane_pick(rows_of, chunks, source) * weight[...]
        payload[:, fields, :] = table[:, 1, :].astype(F32)

    @pl.when(jnp.logical_not(atmos))
    def _():
        payload[...] = jnp.zeros(payload.shape, F32)
        for f in range(fields):
            for at in range(chunks):
                payload[at, f : f + 1, :] = surface[f, 0:1, at * LANES : (at + 1) * LANES]


def back_kernel(got0, got1, got2, table, weight, after, payload):
    comp = lax.axis_index("comp")
    fields = got0.shape[1] - 1
    chunks = 16
    wide = fields + 1

    @pl.when(comp != 3)
    def _():
        source = table[:, 0, :]
        scale = weight[...]
        for f in range(fields):

            def pick(at):
                first, second, third = (got[at, f : f + 1, :] for got in (got0, got1, got2))
                return jnp.where(comp == 0, first, jnp.where(comp == 1, second, third))

            rows = lane_pick(pick, chunks, source)
            payload[:, f, :] = rows * scale
        payload[:, fields, :] = table[:, 1, :].astype(F32)
        payload[:, wide:, :] = jnp.zeros((payload.shape[0], payload.shape[1] - wide, LANES), F32)

    @pl.when(comp == 3)
    def _():
        payload[:, 0:wide, :] = got0[...]
        payload[:, wide : 2 * wide, :] = got1[...]
        payload[:, 2 * wide : 3 * wide, :] = got2[...]


def pick_rims(wanted, parts):
    nodes = parts.shape[1]
    rows = parts.shape[0] // 2
    ids = lax.broadcasted_iota(jnp.int16, (nodes, LANES), 0)
    wanted = jnp.broadcast_to(wanted, (16, LANES)).astype(jnp.int16)
    wanted = jnp.broadcast_to(wanted[None], (nodes // 16, 16, LANES)).reshape(nodes, LANES)
    onehot = jnp.where(ids == wanted, jnp.ones((), BF), jnp.zeros((), BF))
    both = dot(parts[...], onehot)
    return both[:rows] + both[rows:]


def count_links(index, order, target):
    width = target.shape[1]
    one = jnp.ones((16, width), BF)
    zero = jnp.zeros((16, width), BF)
    ids = lax.broadcasted_iota(jnp.int16, (16, width), 0)
    low_off = [
        jnp.broadcast_to(jnp.bitwise_and(row, LANES - 1), (16, width)).astype(jnp.int16) - ids for row in index
    ]
    highs = [jnp.broadcast_to(jnp.right_shift(row, 7), (16, width)).astype(BF) for row in index]
    masks = [[jnp.where(high == block, one, zero) for high in highs] for block in order]
    for sub in range(LANES // 16):
        lows = [jnp.where(off == sub * 16, one, zero) for off in low_off]
        for slot in range(len(order)):
            total = None
            for low, mask in zip(lows, masks[slot]):
                term = low * mask
                total = term if total is None else total + term
            target[slot * LANES + sub * 16 : slot * LANES + sub * 16 + 16, :] = total

def gain_of(ocean, number, metric):
    return OCEAN_RATE * metric if ocean else ATM_STEP / (1.0 + number)

def atmos_field(values, scale, table_high, table_low):
    third = values.shape[0] // 3
    high, low = split(values)
    grads = dot(jnp.concatenate([high, low], axis=1), table_high) + dot(high, table_low)
    grad_xi = grads[:, :LANES]
    grad_eta = grads[:, LANES : 2 * LANES]
    second = grads[:, 2 * LANES :]
    wind_u = jnp.concatenate([values[:third]] * 3, axis=0)
    wind_v = jnp.concatenate([values[third : 2 * third]] * 3, axis=0)
    return (VISCOSITY * scale * scale) * second - scale * (wind_u * grad_xi + wind_v * grad_eta)


def fill_parts(atmos, state, metric, parts, tables):
    rows, nodes = state.shape

    @pl.when(atmos)
    def _():
        high, low = derivative_table()
        tables[:LANES, :] = high
        tables[LANES : 2 * LANES, :] = high
        tables[2 * LANES :, :] = low
        for at in range(nodes // LANES):
            where = slice(at * LANES, (at + 1) * LANES)
            field = atmos_field(state[:, where], metric[0:1, where], tables[: 2 * LANES, :], tables[2 * LANES :, :])
            high, low = split(field)
            parts[0:rows, where] = high
            parts[rows:, where] = low

    @pl.when(jnp.logical_not(atmos))
    def _():
        high, low = split(state[...])
        parts[0:rows, :] = high
        parts[rows:, :] = low


def field_kernel(state, metric, rims, left_ref, right_ref, parts, tables):
    fill_parts(lax.axis_index("comp") != lax.axis_size("comp") - 1, state, metric, parts, tables)
    left_ref[...] = pick_rims(rims[0:1, :], parts)
    right_ref[...] = pick_rims(rims[1:2, :], parts)


def inner_kernel(state, metric, links, column, after, partial, rim_count, gains, column_out, count, parts, tables):
    atmos = lax.axis_index("comp") != lax.axis_size("comp") - 1
    rows, nodes = state.shape
    unroll, _, width = count.shape
    chunks = nodes // LANES
    column_out[...] = column[...]
    fill_parts(atmos, state, metric, parts, tables)

    def run(used, is_ocean):
        def step(at, here):
            where = pl.ds(pl.multiple_of(at * width, width), width)
            index = [links[k, :, where] for k in range(used)]
            number = sum((row >= 0).astype(F32) for row in index)
            count_links(index, list(range(1, chunks + 1)) + [0, chunks + 1], here)
            rim_count[0 : here.shape[0] - nodes, where] = here[nodes:, :]
            both = dot(parts[...], here[0:nodes, :])
            linked = both[:rows] + both[rows:]
            current = state[:, where]
            gain = gain_of(is_ocean, number, metric[0:1, where])
            gains[0:1, where] = gain
            if is_ocean:
                partial[:, where] = current + gain * (linked - number * current)
            else:
                field = parts[0:rows, where].astype(F32) + parts[rows:, where].astype(F32)
                partial[:, where] = current + gain * (field + linked)

        def group(i, carry):
            for u in range(unroll):
                step(i * unroll + u, count.at[u])
            return carry

        lax.fori_loop(0, nodes // width // unroll, group, 0)

    @pl.when(atmos)
    def _():
        run(3, False)

    @pl.when(jnp.logical_not(atmos))
    def _():
        run(6, True)


def final_kernel(
    partial, left, right, got, rim_count, gains, column, result, done, rim_parts, left_rows, onehots, sems
):
    comp = lax.axis_index("comp")
    tile = lax.axis_index("tile")
    last_comp = lax.axis_size("comp") - 1
    last_tile = lax.axis_size("tile") - 1
    ocean = comp == last_comp
    has_left = jnp.logical_not((tile == 0) & (ocean | (comp == 0)))
    has_right = jnp.logical_not((tile == last_tile) & (comp >= last_comp - 1))
    rows, nodes = partial.shape
    levels = column.shape[0]
    senders = got.shape[0]
    rim = left.shape[1]
    width = 2 * LANES
    tiles = nodes // width
    fields = rows // levels
    chunks = nodes // LANES
    ids = lax.broadcasted_iota(jnp.int32, (LANES, LANES), 0)
    ids_high = lax.broadcasted_iota(jnp.int32, (chunks, LANES), 0)

    def land(part, total):
        for a in range(senders):
            base = 4 * part
            cell = got[a, pl.ds(base + fields, 1), :].astype(jnp.int32)
            lane_low = jnp.bitwise_and(cell, LANES - 1)
            lane_high = jnp.right_shift(cell, 7)
            where = slice(a * LANES, (a + 1) * LANES)
            onehots[:, where] = jnp.where(ids == lane_low, 1.0, 0.0).astype(BF)
            mask = ids_high == lane_high
            picked = [jnp.where(mask, got[a, pl.ds(base + f, 1), :], 0.0) for f in range(fields)]
            high, low = split(jnp.concatenate(picked, axis=0))
            left_rows[0 : fields * chunks, where] = high
            left_rows[fields * chunks :, where] = low
        return total + dot_nt(left_rows[...], onehots[...])

    groups = jnp.where(ocean, last_comp, 1)
    landed = lax.fori_loop(0, groups, land, jnp.zeros((2 * fields * chunks, LANES), F32))
    forcing = COUPLING * (landed[: fields * chunks] + landed[fields * chunks :])

    for side, there, source in ((0, has_left, left), (1, has_right, right)):
        high, low = split(jnp.where(there, source[...], 0.0))
        rim_parts[0:rows, side * rim : (side + 1) * rim] = high
        rim_parts[rows:, side * rim : (side + 1) * rim] = low
    col_high, col_low = split(column[...])
    col_gain = column[:, 0:1]
    col = jnp.concatenate([col_high, col_low], axis=0)

    def move(at):
        where = pl.ds(at * width, width)
        return pltpu.make_async_copy(done.at[:, where], result.at[:, where], sems.at[at])

    for at in range(tiles):
        where = slice(at * width, (at + 1) * width)
        both = dot(rim_parts[...], rim_count[0 : 2 * rim, where])
        updated = partial[:, where] + gains[0:1, where] * (both[:rows] + both[rows:])
        uh, ul = split(updated)
        for f in range(fields):
            part = slice(f * levels, (f + 1) * levels)
            full = dot(col, uh[part])
            mixed = full[:levels] + full[levels:] + dot(col_high, ul[part])
            first = f * chunks + at * width // LANES
            rows_of = [forcing[n : n + 1, :] for n in range(first, first + width // LANES)]
            done[part, where] = mixed + col_gain * jnp.concatenate(rows_of, axis=1)
        move(at).start()

    for at in range(tiles):
        move(at).wait()


def call(kernel, args, outs, scratch=(), limit=32, form="vmem", anywhere=(), out_far=(), cost=None):
    free = pl.BlockSpec(memory_space=pl.ANY)
    whole = pl.BlockSpec(memory_space=pltpu.VMEM)

    def spec(dims):
        if form == "block":
            return pl.BlockSpec(dims, lambda i: (0,) * len(dims))
        return free if form == "any" else whole

    params = pltpu.CompilerParams() if limit is None else pltpu.CompilerParams(vmem_limit_bytes=limit * MIB)
    return pl.pallas_call(
        kernel,
        grid=(1,) if form == "block" else (),
        in_specs=[free if n in anywhere else spec(arg.shape) for n, arg in enumerate(args)],
        out_specs=[free if n in out_far else spec(out.shape) for n, out in enumerate(outs)],
        out_shape=outs,
        scratch_shapes=list(scratch),
        compiler_params=params,
        cost_estimate=cost and pl.CostEstimate(flops=cost, bytes_accessed=4_000_000, transcendentals=0),
    )(*args)


def per_device(state, metric, column_op, links, rims, out_map, out_weight, back_map, back_weight):
    _, _, fields, levels, nodes = state.shape
    rows = fields * levels
    rim = rims.shape[-1]
    ntile = lax.axis_size("tile")
    ncomp = lax.axis_size("comp")
    slot = out_map.shape[-1]
    axes = ("comp", "tile")
    total = ncomp * ntile
    chunks = nodes // LANES
    width = 2 * LANES
    tiles = nodes // width
    metric_row = metric.reshape(1, nodes)
    link_rows = links.reshape(6, 1, nodes)
    dma = pltpu.SemaphoreType.DMA
    int32 = jnp.int32

    def shape(*dims, kind=F32):
        return jax.ShapeDtypeStruct(dims, kind)

    def held(*dims, kind=F32):
        return pltpu.VMEM(dims, kind)

    (payload,) = pl.pallas_call(
        out_kernel,
        grid=(1,),
        in_specs=[
            pl.BlockSpec((fields, 8, nodes), lambda i: (0, 0, 0)),
            pl.BlockSpec((ntile, 2, slot), lambda i: (0, 0, 0)),
            pl.BlockSpec((ntile, slot), lambda i: (0, 0)),
        ],
        out_specs=[pl.BlockSpec((ntile, fields + 1, slot), lambda i: (0, 0, 0))],
        out_shape=[shape(ntile, fields + 1, slot)],
    )(state.reshape(fields, levels, nodes), out_map.reshape(ntile, 2, slot), out_weight.reshape(ntile, slot))

    def across(values, flip):
        pairs = [(a * ntile + b, (a ^ flip) * ntile + b) for a in range(ncomp) for b in range(ntile)]
        return lax.ppermute(values, axes, pairs)

    got0 = across(payload, 3)
    got1 = across(payload, 2)
    got2 = across(payload, 1)

    current = state.reshape(rows, nodes)
    to_left, to_right = call(
        field_kernel,
        (current, metric_row, rims.reshape(2, rim)),
        [shape(rows, rim), shape(rows, rim)],
        [held(2 * rows, nodes, kind=BF), held(3 * LANES, 3 * LANES, kind=BF)],

        cost=4_000_000_000,
    )
    steps = [(i, (i + 1) % total) for i in range(total)]
    left = lax.ppermute(to_right, axes, steps)
    right = lax.ppermute(to_left, axes, [(b, a) for a, b in steps])
    (rows_out,) = call(
        back_kernel,
        (got0, got1, got2, back_map.reshape(ntile, 2, slot), back_weight.reshape(ntile, slot), to_left),
        [shape(ntile, (ncomp - 1) * (fields + 1), slot)],
        anywhere=(5,),
    )
    got = lax.all_to_all(rows_out, "tile", split_axis=0, concat_axis=0, tiled=True)

    partial, rim_count, gains, column = call(
        inner_kernel,
        (current, metric_row, link_rows, column_op.reshape(levels, levels), rows_out),
        [shape(rows, nodes), shape(HOLD * rim, nodes, kind=BF), shape(1, nodes), shape(levels, levels)],
        [held(2, nodes + 2 * rim, width, kind=BF), held(2 * rows, nodes, kind=BF), held(3 * LANES, 3 * LANES, kind=BF)],
        anywhere=(4,),
        cost=8_000_000_000,
    )
    (result,) = call(
        final_kernel,
        (partial, left, right, got, rim_count, gains, column),
        [shape(rows, nodes)],
        [
            held(rows, nodes),
            held(2 * rows, 2 * rim, kind=BF),
            held(2 * fields * chunks, ntile * slot, kind=BF),
            held(LANES, ntile * slot, kind=BF),
            dma((tiles,)),
        ],
        out_far=(0,),
    )
    return result.reshape(state.shape)


def solution(mesh):
    return jax.shard_map(
        per_device,
        mesh=mesh,
        in_specs=(
            P("comp", "tile", None, None, None),
            P("comp", "tile", None),
            P("comp", None, None),
            P("comp", "tile", None, None),
            P("comp", "tile", None, None),
            P("comp", "tile", None, None, None),
            P("comp", "tile", None, None),
            P("comp", "tile", None, None, None),
            P("comp", "tile", None, None),
        ),
        out_specs=P("comp", "tile", None, None, None),
        check_vma=False,
    )
```

```python
import math

import jax
import jax.numpy as jnp
import numpy as np
from jax import lax
from jax.experimental import pallas as pl
from jax.experimental.pallas import tpu as pltpu
from jax.sharding import PartitionSpec as P

VISCOSITY = 0.05
ATM_STEP = 0.02
OCEAN_RATE = 0.08
COUPLING = 0.5
LANES = 128
BF = jnp.bfloat16
F32 = jnp.float32
MIB = 1024 * 1024


def gll_matrix():
    points = np.array([-1.0, -1.0 / math.sqrt(5.0), 1.0 / math.sqrt(5.0), 1.0])
    legendre = 0.5 * (5.0 * points * points * points - 3.0 * points)
    matrix = np.zeros((4, 4))
    for a in range(4):
        for b in range(4):
            if a != b:
                matrix[a, b] = legendre[a] / (legendre[b] * (points[a] - points[b]))
    matrix[0, 0] = -3.0
    matrix[3, 3] = 3.0
    return matrix


def derivative_table():
    first = gll_matrix()
    twice = first @ first
    m = lax.broadcasted_iota(jnp.int32, (LANES, LANES), 0)
    n = lax.broadcasted_iota(jnp.int32, (LANES, LANES), 1)

    def entries(a, b, matrices):
        at = jnp.bitwise_and(a, 3) * 4 + jnp.bitwise_and(b, 3)
        values = [jnp.zeros((LANES, LANES), F32) for _ in matrices]
        for row in range(4):
            for column in range(4):
                hit = at == column * 4 + row
                values = [jnp.where(hit, float(p[row, column]), v) for p, v in zip(matrices, values)]
        return values

    same_row = jnp.right_shift(m, 2) == jnp.right_shift(n, 2)
    same_element = jnp.right_shift(m, 4) == jnp.right_shift(n, 4)
    same_column = same_element & (jnp.bitwise_and(m, 3) == jnp.bitwise_and(n, 3))
    xi, xi_twice = entries(m, n, (first, twice))
    eta, eta_twice = entries(jnp.right_shift(m, 2), jnp.right_shift(n, 2), (first, twice))
    parts = [
        jnp.where(same_row, xi, 0.0),
        jnp.where(same_column, eta, 0.0),
        jnp.where(same_row, xi_twice, 0.0) + jnp.where(same_column, eta_twice, 0.0),
    ]
    return split(jnp.concatenate(parts, axis=1))


def split(values):
    high = values.astype(BF)
    low = (values - high.astype(F32)).astype(BF)
    return high, low


def dot(a, b):
    return jnp.dot(a, b, preferred_element_type=F32)


def dot_nt(a, b):
    return lax.dot_general(a, b, (((1,), (1,)), ((), ())), preferred_element_type=F32)


def lane_pick(chunk_of, chunks, index):
    low = jnp.bitwise_and(index, LANES - 1)
    high = jnp.right_shift(index, 7)
    total = jnp.zeros(index.shape, F32)
    for at in range(chunks):
        row = jnp.broadcast_to(chunk_of(at), index.shape)
        picked = jnp.take_along_axis(row, low, axis=1, mode="promise_in_bounds")
        total = jnp.where(high == at, picked, total)
    return total


def out_kernel(surface, table, weight, payload):
    atmos = lax.axis_index("comp") != lax.axis_size("comp") - 1
    fields = surface.shape[0]
    chunks = surface.shape[2] // LANES

    @pl.when(atmos)
    def _():
        source = table[:, 0, :]
        for f in range(fields):
            rows_of = lambda at: surface[f, 0:1, at * LANES : (at + 1) * LANES]
            payload[:, f, :] = lane_pick(rows_of, chunks, source) * weight[...]
        payload[:, fields, :] = table[:, 1, :].astype(F32)

    @pl.when(jnp.logical_not(atmos))
    def _():
        payload[...] = jnp.zeros(payload.shape, F32)
        for f in range(fields):
            for at in range(chunks):
                payload[at, f : f + 1, :] = surface[f, 0:1, at * LANES : (at + 1) * LANES]


def back_kernel(got0, got1, got2, table, weight, after, payload):
    comp = lax.axis_index("comp")
    fields = got0.shape[1] - 1
    chunks = 16
    wide = fields + 1

    @pl.when(comp != 3)
    def _():
        source = table[:, 0, :]
        scale = weight[...]
        for f in range(fields):

            def pick(at):
                first, second, third = (got[at, f : f + 1, :] for got in (got0, got1, got2))
                return jnp.where(comp == 0, first, jnp.where(comp == 1, second, third))

            rows = lane_pick(pick, chunks, source)
            payload[:, f, :] = rows * scale
        payload[:, fields, :] = table[:, 1, :].astype(F32)
        payload[:, wide:, :] = jnp.zeros((payload.shape[0], payload.shape[1] - wide, LANES), F32)

    @pl.when(comp == 3)
    def _():
        payload[:, 0:wide, :] = got0[...]
        payload[:, wide : 2 * wide, :] = got1[...]
        payload[:, 2 * wide : 3 * wide, :] = got2[...]


def pick_rims(wanted, parts):
    nodes = parts.shape[1]
    rows = parts.shape[0] // 2
    ids = lax.broadcasted_iota(jnp.int16, (nodes, LANES), 0)
    wanted = jnp.broadcast_to(wanted, (16, LANES)).astype(jnp.int16)
    wanted = jnp.broadcast_to(wanted[None], (nodes // 16, 16, LANES)).reshape(nodes, LANES)
    onehot = jnp.where(ids == wanted, jnp.ones((), BF), jnp.zeros((), BF))
    both = dot(parts[...], onehot)
    return both[:rows] + both[rows:]


def count_links(index, order, target):
    width = target.shape[1]
    one = jnp.ones((16, width), BF)
    zero = jnp.zeros((16, width), BF)
    ids = lax.broadcasted_iota(jnp.int16, (16, width), 0)
    low_off = [
        jnp.broadcast_to(jnp.bitwise_and(row, LANES - 1), (16, width)).astype(jnp.int16) - ids for row in index
    ]
    highs = [jnp.broadcast_to(jnp.right_shift(row, 7), (16, width)).astype(BF) for row in index]
    masks = [[jnp.where(high == block, one, zero) for high in highs] for block in order]
    for sub in range(LANES // 16):
        lows = [jnp.where(off == sub * 16, one, zero) for off in low_off]
        for slot in range(len(order)):
            total = None
            for low, mask in zip(lows, masks[slot]):
                term = low * mask
                total = term if total is None else total + term
            target[slot * LANES + sub * 16 : slot * LANES + sub * 16 + 16, :] = total

def gain_of(ocean, number, metric):
    return OCEAN_RATE * metric if ocean else ATM_STEP / (1.0 + number)

def atmos_field(values, scale, table_high, table_low):
    third = values.shape[0] // 3
    high, low = split(values)
    grads = dot(jnp.concatenate([high, low], axis=1), table_high) + dot(high, table_low)
    grad_xi = grads[:, :LANES]
    grad_eta = grads[:, LANES : 2 * LANES]
    second = grads[:, 2 * LANES :]
    wind_u = jnp.concatenate([values[:third]] * 3, axis=0)
    wind_v = jnp.concatenate([values[third : 2 * third]] * 3, axis=0)
    return (VISCOSITY * scale * scale) * second - scale * (wind_u * grad_xi + wind_v * grad_eta)


def fill_parts(atmos, state, metric, parts, tables):
    rows, nodes = state.shape

    @pl.when(atmos)
    def _():
        high, low = derivative_table()
        tables[:LANES, :] = high
        tables[LANES : 2 * LANES, :] = high
        tables[2 * LANES :, :] = low
        for at in range(nodes // LANES):
            where = slice(at * LANES, (at + 1) * LANES)
            field = atmos_field(state[:, where], metric[0:1, where], tables[: 2 * LANES, :], tables[2 * LANES :, :])
            high, low = split(field)
            parts[0:rows, where] = high
            parts[rows:, where] = low

    @pl.when(jnp.logical_not(atmos))
    def _():
        high, low = split(state[...])
        parts[0:rows, :] = high
        parts[rows:, :] = low


def field_kernel(state, metric, rims, state_here, left_ref, right_ref, parts, tables):
    state_here[...] = state[...]
    fill_parts(lax.axis_index("comp") != lax.axis_size("comp") - 1, state, metric, parts, tables)
    left_ref[...] = pick_rims(rims[0:1, :], parts)
    right_ref[...] = pick_rims(rims[1:2, :], parts)


def inner_kernel(state, metric, links, column, after, partial, gains, links_out, column_out, count, parts, tables):
    atmos = lax.axis_index("comp") != lax.axis_size("comp") - 1
    rows, nodes = state.shape
    unroll, _, width = count.shape
    chunks = nodes // LANES
    column_out[...] = column[...]
    links_out[...] = links[...]
    fill_parts(atmos, state, metric, parts, tables)

    def run(used, is_ocean):
        def step(at, here):
            where = pl.ds(pl.multiple_of(at * width, width), width)
            index = [links[k, :, where] for k in range(used)]
            number = sum((row >= 0).astype(F32) for row in index)
            count_links(index, list(range(1, chunks + 1)), here)
            both = dot(parts[...], here[...])
            linked = both[:rows] + both[rows:]
            current = state[:, where]
            gain = gain_of(is_ocean, number, metric[0:1, where])
            gains[0:1, where] = gain
            if is_ocean:
                partial[:, where] = current + gain * (linked - number * current)
            else:
                field = parts[0:rows, where].astype(F32) + parts[rows:, where].astype(F32)
                partial[:, where] = current + gain * (field + linked)

        def group(i, carry):
            for u in range(unroll):
                step(i * unroll + u, count.at[u])
            return carry

        lax.fori_loop(0, nodes // width // unroll, group, 0)

    @pl.when(atmos)
    def _():
        run(3, False)

    @pl.when(jnp.logical_not(atmos))
    def _():
        run(6, True)


def final_kernel(
    partial, left, right, got, gains, links, column, result, done, rim_parts, left_rows, onehots, count, wide, sems
):
    comp = lax.axis_index("comp")
    tile = lax.axis_index("tile")
    last_comp = lax.axis_size("comp") - 1
    last_tile = lax.axis_size("tile") - 1
    ocean = comp == last_comp
    has_left = jnp.logical_not((tile == 0) & (ocean | (comp == 0)))
    has_right = jnp.logical_not((tile == last_tile) & (comp >= last_comp - 1))
    rows, nodes = partial.shape
    levels = column.shape[0]
    senders = got.shape[0]
    rim = left.shape[1]
    width = 2 * LANES
    tiles = nodes // width
    fields = rows // levels
    chunks = nodes // LANES
    ids = lax.broadcasted_iota(jnp.int16, (LANES, LANES), 0)
    ids_high = lax.broadcasted_iota(jnp.int16, (chunks, LANES), 0)
    one = jnp.ones((), BF)
    zero = jnp.zeros((), BF)

    def land(part, total):
        for a in range(senders):
            base_row = 4 * part
            cell = got[a, pl.ds(base_row + fields, 1), :].astype(jnp.int32)
            lane_low = jnp.broadcast_to(jnp.bitwise_and(cell, LANES - 1), (chunks, LANES)).astype(jnp.int16)
            lane_high = jnp.broadcast_to(jnp.right_shift(cell, 7), (chunks, LANES)).astype(jnp.int16)
            wanted = jnp.broadcast_to(lane_low[None], (LANES // chunks, chunks, LANES)).reshape(LANES, LANES)
            where = slice(a * LANES, (a + 1) * LANES)
            onehots[:, where] = jnp.where(ids == wanted, one, zero)
            mask = ids_high == lane_high
            for f in range(fields):
                row = got[a, pl.ds(base_row + f, 1), :]
                high = row.astype(BF).astype(F32)
                for n, value in ((f, high), (fields + f, row - high)):
                    spread = jnp.broadcast_to(value, (chunks, LANES)).astype(BF)
                    left_rows[n * chunks : (n + 1) * chunks, where] = jnp.where(mask, spread, zero)
        return total + dot_nt(left_rows[...], onehots[...])

    groups = jnp.where(ocean, last_comp, 1)
    landed = lax.fori_loop(0, groups, land, jnp.zeros((2 * fields * chunks, LANES), F32))
    forcing = COUPLING * (landed[: fields * chunks] + landed[fields * chunks :])

    for side, there, source in ((0, has_left, left), (1, has_right, right)):
        high, low = split(jnp.where(there, source[...], 0.0))
        rim_parts[0:rows, side * rim : (side + 1) * rim] = high
        rim_parts[rows:, side * rim : (side + 1) * rim] = low
    wide[...] = jnp.zeros(wide.shape, F32)
    for f in range(fields):
        at = f * levels
        wide[at : at + levels, at : at + levels] = column[...]
    col_high, col_low = split(wide[:, 0:rows])
    col = jnp.concatenate([col_high, col_low], axis=0)
    col_gain = column[:, 0:1]

    def move(at):
        where = pl.ds(at * width, width)
        return pltpu.make_async_copy(done.at[:, where], result.at[:, where], sems.at[at])

    def run(used):
        for at in range(tiles):
            where = slice(at * width, (at + 1) * width)
            here = count.at[at % 2]
            count_links([links[k, :, where] for k in range(used)], [0, chunks + 1], here)
            both = dot(rim_parts[...], here[...])
            updated = partial[:, where] + gains[0:1, where] * (both[:rows] + both[rows:])
            high, low = split(updated)
            full = dot(col, high)
            mixed = full[:rows] + full[rows:] + dot(col_high, low)
            for f in range(fields):
                part = slice(f * levels, (f + 1) * levels)
                first = f * chunks + at * width // LANES
                rows_of = [forcing[n : n + 1, :] for n in range(first, first + width // LANES)]
                done[part, where] = mixed[part] + col_gain * jnp.concatenate(rows_of, axis=1)
            move(at).start()

    @pl.when(jnp.logical_not(ocean))
    def _():
        run(3)

    @pl.when(ocean)
    def _():
        run(6)

    for at in range(tiles):
        move(at).wait()


def call(kernel, args, outs, scratch=(), limit=32, form="vmem", anywhere=(), out_far=(), cost=None, alias=None):
    free = pl.BlockSpec(memory_space=pl.ANY)
    whole = pl.BlockSpec(memory_space=pltpu.VMEM)

    def spec(dims):
        if form == "block":
            return pl.BlockSpec(dims, lambda i: (0,) * len(dims))
        return free if form == "any" else whole

    params = pltpu.CompilerParams() if limit is None else pltpu.CompilerParams(vmem_limit_bytes=limit * MIB)
    return pl.pallas_call(
        kernel,
        grid=(1,) if form == "block" else (),
        in_specs=[free if n in anywhere else spec(arg.shape) for n, arg in enumerate(args)],
        out_specs=[free if n in out_far else spec(out.shape) for n, out in enumerate(outs)],
        out_shape=outs,
        scratch_shapes=list(scratch),
        compiler_params=params,
        input_output_aliases=alias or {},
        cost_estimate=cost and pl.CostEstimate(flops=cost, bytes_accessed=4_000_000, transcendentals=0),
    )(*args)


def per_device(state, metric, column_op, links, rims, out_map, out_weight, back_map, back_weight):
    _, _, fields, levels, nodes = state.shape
    rows = fields * levels
    rim = rims.shape[-1]
    ntile = lax.axis_size("tile")
    ncomp = lax.axis_size("comp")
    slot = out_map.shape[-1]
    axes = ("comp", "tile")
    total = ncomp * ntile
    chunks = nodes // LANES
    width = 2 * LANES
    tiles = nodes // width
    metric_row = metric.reshape(1, nodes)
    link_rows = links.reshape(6, 1, nodes)
    dma = pltpu.SemaphoreType.DMA
    int32 = jnp.int32

    def shape(*dims, kind=F32):
        return jax.ShapeDtypeStruct(dims, kind)

    def held(*dims, kind=F32):
        return pltpu.VMEM(dims, kind)

    (payload,) = pl.pallas_call(
        out_kernel,
        grid=(1,),
        in_specs=[
            pl.BlockSpec((fields, 8, nodes), lambda i: (0, 0, 0)),
            pl.BlockSpec((ntile, 2, slot), lambda i: (0, 0, 0)),
            pl.BlockSpec((ntile, slot), lambda i: (0, 0)),
        ],
        out_specs=[pl.BlockSpec((ntile, fields + 1, slot), lambda i: (0, 0, 0))],
        out_shape=[shape(ntile, fields + 1, slot)],
    )(state.reshape(fields, levels, nodes), out_map.reshape(ntile, 2, slot), out_weight.reshape(ntile, slot))

    def across(values, flip):
        pairs = [(a * ntile + b, (a ^ flip) * ntile + b) for a in range(ncomp) for b in range(ntile)]
        return lax.ppermute(values, axes, pairs)

    got0 = across(payload, 3)
    got1 = across(payload, 2)
    got2 = across(payload, 1)

    current = state.reshape(rows, nodes)
    state_here, to_left, to_right = call(
        field_kernel,
        (current, metric_row, rims.reshape(2, rim)),
        [shape(rows, nodes), shape(rows, rim), shape(rows, rim)],
        [held(2 * rows, nodes, kind=BF), held(3 * LANES, 3 * LANES, kind=BF)],

        cost=4_000_000_000,
    )
    steps = [(i, (i + 1) % total) for i in range(total)]
    left = lax.ppermute(to_right, axes, steps)
    right = lax.ppermute(to_left, axes, [(b, a) for a, b in steps])
    (rows_out,) = call(
        back_kernel,
        (got0, got1, got2, back_map.reshape(ntile, 2, slot), back_weight.reshape(ntile, slot), to_right),
        [shape(ntile, (ncomp - 1) * (fields + 1), slot)],
        anywhere=(5,),
    )
    got = lax.all_to_all(rows_out, "tile", split_axis=0, concat_axis=0, tiled=True)

    partial, gains, links_here, column = call(
        inner_kernel,
        (state_here, metric_row, link_rows, column_op.reshape(levels, levels), rows_out),
        [shape(rows, nodes), shape(1, nodes), shape(6, 1, nodes, kind=int32), shape(levels, levels)],
        [held(2, nodes, width, kind=BF), held(2 * rows, nodes, kind=BF), held(3 * LANES, 3 * LANES, kind=BF)],
        anywhere=(4,),
        cost=8_000_000_000,
        alias={0: 0},
    )
    (result,) = call(
        final_kernel,
        (partial, left, right, got, gains, links_here, column),
        [shape(rows, nodes)],
        [
            held(rows, nodes),
            held(2 * rows, 2 * rim, kind=BF),
            held(2 * fields * chunks, ntile * slot, kind=BF),
            held(LANES, ntile * slot, kind=BF),
            held(2, 2 * rim, width, kind=BF),
            held(rows, width),
            dma((tiles,)),
        ],
        out_far=(0,),
    )
    return result.reshape(state.shape)


def solution(mesh):
    return jax.shard_map(
        per_device,
        mesh=mesh,
        in_specs=(
            P("comp", "tile", None, None, None),
            P("comp", "tile", None),
            P("comp", None, None),
            P("comp", "tile", None, None),
            P("comp", "tile", None, None),
            P("comp", "tile", None, None, None),
            P("comp", "tile", None, None),
            P("comp", "tile", None, None, None),
            P("comp", "tile", None, None),
        ),
        out_specs=P("comp", "tile", None, None, None),
        check_vma=False,
    )
```

```python
import math

import jax
import jax.numpy as jnp
import numpy as np
from jax import lax
from jax.experimental import pallas as pl
from jax.experimental.pallas import tpu as pltpu
from jax.sharding import PartitionSpec as P

VISCOSITY = 0.05
ATM_STEP = 0.02
OCEAN_RATE = 0.08
COUPLING = 0.5
LANES = 128
BF = jnp.bfloat16
F32 = jnp.float32
MIB = 1024 * 1024


def gll_matrix():
    points = np.array([-1.0, -1.0 / math.sqrt(5.0), 1.0 / math.sqrt(5.0), 1.0])
    legendre = 0.5 * (5.0 * points * points * points - 3.0 * points)
    matrix = np.zeros((4, 4))
    for a in range(4):
        for b in range(4):
            if a != b:
                matrix[a, b] = legendre[a] / (legendre[b] * (points[a] - points[b]))
    matrix[0, 0] = -3.0
    matrix[3, 3] = 3.0
    return matrix


def derivative_table():
    first = gll_matrix()
    twice = first @ first
    m = lax.broadcasted_iota(jnp.int32, (LANES, LANES), 0)
    n = lax.broadcasted_iota(jnp.int32, (LANES, LANES), 1)

    def entries(a, b, matrices):
        at = jnp.bitwise_and(a, 3) * 4 + jnp.bitwise_and(b, 3)
        values = [jnp.zeros((LANES, LANES), F32) for _ in matrices]
        for row in range(4):
            for column in range(4):
                hit = at == column * 4 + row
                values = [jnp.where(hit, float(p[row, column]), v) for p, v in zip(matrices, values)]
        return values

    same_row = jnp.right_shift(m, 2) == jnp.right_shift(n, 2)
    same_element = jnp.right_shift(m, 4) == jnp.right_shift(n, 4)
    same_column = same_element & (jnp.bitwise_and(m, 3) == jnp.bitwise_and(n, 3))
    xi, xi_twice = entries(m, n, (first, twice))
    eta, eta_twice = entries(jnp.right_shift(m, 2), jnp.right_shift(n, 2), (first, twice))
    parts = [
        jnp.where(same_row, xi, 0.0),
        jnp.where(same_column, eta, 0.0),
        jnp.where(same_row, xi_twice, 0.0) + jnp.where(same_column, eta_twice, 0.0),
    ]
    return split(jnp.concatenate(parts, axis=1))


def split(values):
    high = values.astype(BF)
    low = (values - high.astype(F32)).astype(BF)
    return high, low


def dot(a, b):
    return jnp.dot(a, b, preferred_element_type=F32)


def dot_nt(a, b):
    return lax.dot_general(a, b, (((1,), (1,)), ((), ())), preferred_element_type=F32)


def lane_pick(chunk_of, chunks, index):
    low = jnp.bitwise_and(index, LANES - 1)
    high = jnp.right_shift(index, 7)
    total = jnp.zeros(index.shape, F32)
    for at in range(chunks):
        row = jnp.broadcast_to(chunk_of(at), index.shape)
        picked = jnp.take_along_axis(row, low, axis=1, mode="promise_in_bounds")
        total = jnp.where(high == at, picked, total)
    return total


def out_kernel(surface, table, weight, payload):
    atmos = lax.axis_index("comp") != lax.axis_size("comp") - 1
    fields = surface.shape[0]
    chunks = surface.shape[2] // LANES

    @pl.when(atmos)
    def _():
        source = table[:, 0, :]
        for f in range(fields):
            rows_of = lambda at: surface[f, 0:1, at * LANES : (at + 1) * LANES]
            payload[:, f, :] = lane_pick(rows_of, chunks, source) * weight[...]
        payload[:, fields, :] = table[:, 1, :].astype(F32)

    @pl.when(jnp.logical_not(atmos))
    def _():
        payload[...] = jnp.zeros(payload.shape, F32)
        for f in range(fields):
            for at in range(chunks):
                payload[at, f : f + 1, :] = surface[f, 0:1, at * LANES : (at + 1) * LANES]


def back_kernel(got0, got1, got2, table, weight, after, payload):
    comp = lax.axis_index("comp")
    fields = got0.shape[1] - 1
    chunks = 16
    wide = fields + 1

    @pl.when(comp != 3)
    def _():
        source = table[:, 0, :]
        scale = weight[...]
        for f in range(fields):

            def pick(at):
                first, second, third = (got[at, f : f + 1, :] for got in (got0, got1, got2))
                return jnp.where(comp == 0, first, jnp.where(comp == 1, second, third))

            rows = lane_pick(pick, chunks, source)
            payload[:, f, :] = rows * scale
        payload[:, fields, :] = table[:, 1, :].astype(F32)
        payload[:, wide:, :] = jnp.zeros((payload.shape[0], payload.shape[1] - wide, LANES), F32)

    @pl.when(comp == 3)
    def _():
        payload[:, 0:wide, :] = got0[...]
        payload[:, wide : 2 * wide, :] = got1[...]
        payload[:, 2 * wide : 3 * wide, :] = got2[...]


def pick_rims(wanted, parts):
    nodes = parts.shape[1]
    rows = parts.shape[0] // 2
    ids = lax.broadcasted_iota(jnp.int16, (nodes, LANES), 0)
    wanted = jnp.broadcast_to(wanted, (16, LANES)).astype(jnp.int16)
    wanted = jnp.broadcast_to(wanted[None], (nodes // 16, 16, LANES)).reshape(nodes, LANES)
    onehot = jnp.where(ids == wanted, jnp.ones((), BF), jnp.zeros((), BF))
    both = dot(parts[...], onehot)
    return both[:rows] + both[rows:]


def count_links(index, order, target):
    width = target.shape[1]
    one = jnp.ones((16, width), BF)
    zero = jnp.zeros((16, width), BF)
    ids = lax.broadcasted_iota(jnp.int16, (16, width), 0)
    low_off = [
        jnp.broadcast_to(jnp.bitwise_and(row, LANES - 1), (16, width)).astype(jnp.int16) - ids for row in index
    ]
    highs = [jnp.broadcast_to(jnp.right_shift(row, 7), (16, width)).astype(BF) for row in index]
    masks = [[jnp.where(high == block, one, zero) for high in highs] for block in order]
    for sub in range(LANES // 16):
        lows = [jnp.where(off == sub * 16, one, zero) for off in low_off]
        for slot in range(len(order)):
            total = None
            for low, mask in zip(lows, masks[slot]):
                term = low * mask
                total = term if total is None else total + term
            target[slot * LANES + sub * 16 : slot * LANES + sub * 16 + 16, :] = total

def gain_of(ocean, number, metric):
    return OCEAN_RATE * metric if ocean else ATM_STEP / (1.0 + number)

def atmos_field(values, scale, table_high, table_low):
    third = values.shape[0] // 3
    high, low = split(values)
    grads = dot(jnp.concatenate([high, low], axis=1), table_high) + dot(high, table_low)
    grad_xi = grads[:, :LANES]
    grad_eta = grads[:, LANES : 2 * LANES]
    second = grads[:, 2 * LANES :]
    wind_u = jnp.concatenate([values[:third]] * 3, axis=0)
    wind_v = jnp.concatenate([values[third : 2 * third]] * 3, axis=0)
    return (VISCOSITY * scale * scale) * second - scale * (wind_u * grad_xi + wind_v * grad_eta)


def fill_parts(atmos, state, metric, parts, tables):
    rows, nodes = state.shape

    @pl.when(atmos)
    def _():
        high, low = derivative_table()
        tables[:LANES, :] = high
        tables[LANES : 2 * LANES, :] = high
        tables[2 * LANES :, :] = low
        for at in range(nodes // LANES):
            where = slice(at * LANES, (at + 1) * LANES)
            field = atmos_field(state[:, where], metric[0:1, where], tables[: 2 * LANES, :], tables[2 * LANES :, :])
            high, low = split(field)
            parts[0:rows, where] = high
            parts[rows:, where] = low

    @pl.when(jnp.logical_not(atmos))
    def _():
        high, low = split(state[...])
        parts[0:rows, :] = high
        parts[rows:, :] = low


def field_kernel(state, metric, rims, state_here, left_ref, right_ref, parts, tables):
    state_here[...] = state[...]
    fill_parts(lax.axis_index("comp") != lax.axis_size("comp") - 1, state, metric, parts, tables)
    left_ref[...] = pick_rims(rims[0:1, :], parts)
    right_ref[...] = pick_rims(rims[1:2, :], parts)


def inner_kernel(state, metric, links, column, after, partial, gains, links_out, column_out, count, parts, tables):
    atmos = lax.axis_index("comp") != lax.axis_size("comp") - 1
    rows, nodes = state.shape
    unroll, _, width = count.shape
    chunks = nodes // LANES
    column_out[...] = column[...]
    links_out[...] = links[...]
    fill_parts(atmos, state, metric, parts, tables)

    def run(used, is_ocean):
        def step(at, here):
            where = pl.ds(pl.multiple_of(at * width, width), width)
            index = [links[k, :, where] for k in range(used)]
            number = sum((row >= 0).astype(F32) for row in index)
            count_links(index, list(range(1, chunks + 1)), here)
            both = dot(parts[...], here[...])
            linked = both[:rows] + both[rows:]
            current = state[:, where]
            gain = gain_of(is_ocean, number, metric[0:1, where])
            gains[0:1, where] = gain
            if is_ocean:
                partial[:, where] = current + gain * (linked - number * current)
            else:
                field = parts[0:rows, where].astype(F32) + parts[rows:, where].astype(F32)
                partial[:, where] = current + gain * (field + linked)

        def group(i, carry):
            for u in range(unroll):
                step(i * unroll + u, count.at[u])
            return carry

        lax.fori_loop(0, nodes // width // unroll, group, 0)

    @pl.when(atmos)
    def _():
        run(3, False)

    @pl.when(jnp.logical_not(atmos))
    def _():
        run(6, True)


def rim_kernel(partial, left, right, gains, links, column, mixed, column_out, rim_parts, count, wide):
    comp = lax.axis_index("comp")
    tile = lax.axis_index("tile")
    last_comp = lax.axis_size("comp") - 1
    last_tile = lax.axis_size("tile") - 1
    ocean = comp == last_comp
    has_left = jnp.logical_not((tile == 0) & (ocean | (comp == 0)))
    has_right = jnp.logical_not((tile == last_tile) & (comp >= last_comp - 1))
    rows, nodes = partial.shape
    levels = column.shape[0]
    rim = left.shape[1]
    width = 2 * LANES
    chunks = nodes // LANES
    column_out[...] = column[...]
    for side, there, source in ((0, has_left, left), (1, has_right, right)):
        high, low = split(jnp.where(there, source[...], 0.0))
        rim_parts[0:rows, side * rim : (side + 1) * rim] = high
        rim_parts[rows:, side * rim : (side + 1) * rim] = low
    wide[...] = jnp.zeros(wide.shape, F32)
    for f in range(rows // levels):
        at = f * levels
        wide[at : at + levels, at : at + levels] = column[...]
    col_high, col_low = split(wide[:, 0:rows])
    col = jnp.concatenate([col_high, col_low], axis=0)

    def run(used):
        for at in range(nodes // width):
            where = slice(at * width, (at + 1) * width)
            here = count.at[at % 2]
            count_links([links[k, :, where] for k in range(used)], [0, chunks + 1], here)
            both = dot(rim_parts[...], here[...])
            updated = partial[:, where] + gains[0:1, where] * (both[:rows] + both[rows:])
            high, low = split(updated)
            full = dot(col, high)
            mixed[:, where] = full[:rows] + full[rows:] + dot(col_high, low)

    @pl.when(jnp.logical_not(ocean))
    def _():
        run(3)

    @pl.when(ocean)
    def _():
        run(6)


def final_kernel(mixed, got, column, result, done, left_rows, onehots, sems):
    last_comp = lax.axis_size("comp") - 1
    ocean = lax.axis_index("comp") == last_comp
    rows, nodes = mixed.shape
    levels = column.shape[0]
    senders = got.shape[0]
    width = 2 * LANES
    tiles = nodes // width
    fields = rows // levels
    chunks = nodes // LANES
    ids = lax.broadcasted_iota(jnp.int16, (LANES, LANES), 0)
    ids_high = lax.broadcasted_iota(jnp.int16, (chunks, LANES), 0)
    one = jnp.ones((), BF)
    zero = jnp.zeros((), BF)

    def land(part, total):
        for a in range(senders):
            base_row = 4 * part
            cell = got[a, pl.ds(base_row + fields, 1), :].astype(jnp.int32)
            lane_low = jnp.broadcast_to(jnp.bitwise_and(cell, LANES - 1), (chunks, LANES)).astype(jnp.int16)
            lane_high = jnp.broadcast_to(jnp.right_shift(cell, 7), (chunks, LANES)).astype(jnp.int16)
            wanted = jnp.broadcast_to(lane_low[None], (LANES // chunks, chunks, LANES)).reshape(LANES, LANES)
            where = slice(a * LANES, (a + 1) * LANES)
            onehots[:, where] = jnp.where(ids == wanted, one, zero)
            mask = ids_high == lane_high
            for f in range(fields):
                row = got[a, pl.ds(base_row + f, 1), :]
                high = row.astype(BF).astype(F32)
                for n, value in ((f, high), (fields + f, row - high)):
                    spread = jnp.broadcast_to(value, (chunks, LANES)).astype(BF)
                    left_rows[n * chunks : (n + 1) * chunks, where] = jnp.where(mask, spread, zero)
        return total + dot_nt(left_rows[...], onehots[...])

    groups = jnp.where(ocean, last_comp, 1)
    landed = lax.fori_loop(0, groups, land, jnp.zeros((2 * fields * chunks, LANES), F32))
    forcing = COUPLING * (landed[: fields * chunks] + landed[fields * chunks :])

    col_gain = jnp.broadcast_to(column[:, 0:1], (levels, width))

    def move(at):
        where = pl.ds(at * width, width)
        return pltpu.make_async_copy(done.at[:, where], result.at[:, where], sems.at[at])

    for at in range(tiles):
        where = slice(at * width, (at + 1) * width)
        for f in range(fields):
            part = slice(f * levels, (f + 1) * levels)
            first = f * chunks + at * width // LANES
            rows_of = [forcing[n : n + 1, :] for n in range(first, first + width // LANES)]
            done[part, where] = mixed[part, where] + col_gain * jnp.concatenate(rows_of, axis=1)
        move(at).start()

    for at in range(tiles):
        move(at).wait()


def call(kernel, args, outs, scratch=(), limit=32, form="vmem", anywhere=(), out_far=(), cost=None, alias=None):
    free = pl.BlockSpec(memory_space=pl.ANY)
    whole = pl.BlockSpec(memory_space=pltpu.VMEM)

    def spec(dims):
        if form == "block":
            return pl.BlockSpec(dims, lambda i: (0,) * len(dims))
        return free if form == "any" else whole

    params = pltpu.CompilerParams() if limit is None else pltpu.CompilerParams(vmem_limit_bytes=limit * MIB)
    return pl.pallas_call(
        kernel,
        grid=(1,) if form == "block" else (),
        in_specs=[free if n in anywhere else spec(arg.shape) for n, arg in enumerate(args)],
        out_specs=[free if n in out_far else spec(out.shape) for n, out in enumerate(outs)],
        out_shape=outs,
        scratch_shapes=list(scratch),
        compiler_params=params,
        input_output_aliases=alias or {},
        cost_estimate=cost and pl.CostEstimate(flops=cost, bytes_accessed=4_000_000, transcendentals=0),
    )(*args)


def per_device(state, metric, column_op, links, rims, out_map, out_weight, back_map, back_weight):
    _, _, fields, levels, nodes = state.shape
    rows = fields * levels
    rim = rims.shape[-1]
    ntile = lax.axis_size("tile")
    ncomp = lax.axis_size("comp")
    slot = out_map.shape[-1]
    axes = ("comp", "tile")
    total = ncomp * ntile
    chunks = nodes // LANES
    width = 2 * LANES
    tiles = nodes // width
    metric_row = metric.reshape(1, nodes)
    link_rows = links.reshape(6, 1, nodes)
    dma = pltpu.SemaphoreType.DMA
    int32 = jnp.int32

    def shape(*dims, kind=F32):
        return jax.ShapeDtypeStruct(dims, kind)

    def held(*dims, kind=F32):
        return pltpu.VMEM(dims, kind)

    (payload,) = pl.pallas_call(
        out_kernel,
        grid=(1,),
        in_specs=[
            pl.BlockSpec((fields, 8, nodes), lambda i: (0, 0, 0)),
            pl.BlockSpec((ntile, 2, slot), lambda i: (0, 0, 0)),
            pl.BlockSpec((ntile, slot), lambda i: (0, 0)),
        ],
        out_specs=[pl.BlockSpec((ntile, fields + 1, slot), lambda i: (0, 0, 0))],
        out_shape=[shape(ntile, fields + 1, slot)],
    )(state.reshape(fields, levels, nodes), out_map.reshape(ntile, 2, slot), out_weight.reshape(ntile, slot))

    def across(values, flip):
        pairs = [(a * ntile + b, (a ^ flip) * ntile + b) for a in range(ncomp) for b in range(ntile)]
        return lax.ppermute(values, axes, pairs)

    got0 = across(payload, 3)
    got1 = across(payload, 2)
    got2 = across(payload, 1)

    current = state.reshape(rows, nodes)
    state_here, to_left, to_right = call(
        field_kernel,
        (current, metric_row, rims.reshape(2, rim)),
        [shape(rows, nodes), shape(rows, rim), shape(rows, rim)],
        [held(2 * rows, nodes, kind=BF), held(3 * LANES, 3 * LANES, kind=BF)],

        cost=4_000_000_000,
    )
    steps = [(i, (i + 1) % total) for i in range(total)]
    left = lax.ppermute(to_right, axes, steps)
    right = lax.ppermute(to_left, axes, [(b, a) for a, b in steps])
    (rows_out,) = call(
        back_kernel,
        (got0, got1, got2, back_map.reshape(ntile, 2, slot), back_weight.reshape(ntile, slot), to_right),
        [shape(ntile, (ncomp - 1) * (fields + 1), slot)],
        anywhere=(5,),
    )
    got = lax.all_to_all(rows_out, "tile", split_axis=0, concat_axis=0, tiled=True)

    partial, gains, links_here, column = call(
        inner_kernel,
        (state_here, metric_row, link_rows, column_op.reshape(levels, levels), rows_out),
        [shape(rows, nodes), shape(1, nodes), shape(6, 1, nodes, kind=int32), shape(levels, levels)],
        [held(4, nodes, width, kind=BF), held(2 * rows, nodes, kind=BF), held(3 * LANES, 3 * LANES, kind=BF)],
        anywhere=(4,),
        cost=8_000_000_000,
        alias={0: 0},
    )
    mixed, column = call(
        rim_kernel,
        (partial, left, right, gains, links_here, column),
        [shape(rows, nodes), shape(levels, levels)],
        [held(2 * rows, 2 * rim, kind=BF), held(2, 2 * rim, width, kind=BF), held(rows, width)],
        alias={0: 0},
    )
    (result,) = call(
        final_kernel,
        (mixed, got, column),
        [shape(rows, nodes)],
        [
            held(rows, nodes),
            held(2 * fields * chunks, ntile * slot, kind=BF),
            held(LANES, ntile * slot, kind=BF),
            dma((tiles,)),
        ],
        out_far=(0,),
    )
    return result.reshape(state.shape)


def solution(mesh):
    return jax.shard_map(
        per_device,
        mesh=mesh,
        in_specs=(
            P("comp", "tile", None, None, None),
            P("comp", "tile", None),
            P("comp", None, None),
            P("comp", "tile", None, None),
            P("comp", "tile", None, None),
            P("comp", "tile", None, None, None),
            P("comp", "tile", None, None),
            P("comp", "tile", None, None, None),
            P("comp", "tile", None, None),
        ),
        out_specs=P("comp", "tile", None, None, None),
        check_vma=False,
    )
```

```python
import math

import jax
import jax.numpy as jnp
import numpy as np
from jax import lax
from jax.experimental import pallas as pl
from jax.experimental.pallas import tpu as pltpu
from jax.sharding import PartitionSpec as P

VISCOSITY = 0.05
ATM_STEP = 0.02
OCEAN_RATE = 0.08
COUPLING = 0.5
LANES = 128
BF = jnp.bfloat16
F32 = jnp.float32
MIB = 1024 * 1024


def gll_matrix():
    points = np.array([-1.0, -1.0 / math.sqrt(5.0), 1.0 / math.sqrt(5.0), 1.0])
    legendre = 0.5 * (5.0 * points * points * points - 3.0 * points)
    matrix = np.zeros((4, 4))
    for a in range(4):
        for b in range(4):
            if a != b:
                matrix[a, b] = legendre[a] / (legendre[b] * (points[a] - points[b]))
    matrix[0, 0] = -3.0
    matrix[3, 3] = 3.0
    return matrix


def derivative_table():
    first = gll_matrix()
    twice = first @ first
    m = lax.broadcasted_iota(jnp.int32, (LANES, LANES), 0)
    n = lax.broadcasted_iota(jnp.int32, (LANES, LANES), 1)

    def entries(a, b, matrices):
        at = jnp.bitwise_and(a, 3) * 4 + jnp.bitwise_and(b, 3)
        values = [jnp.zeros((LANES, LANES), F32) for _ in matrices]
        for row in range(4):
            for column in range(4):
                hit = at == column * 4 + row
                values = [jnp.where(hit, float(p[row, column]), v) for p, v in zip(matrices, values)]
        return values

    same_row = jnp.right_shift(m, 2) == jnp.right_shift(n, 2)
    same_element = jnp.right_shift(m, 4) == jnp.right_shift(n, 4)
    same_column = same_element & (jnp.bitwise_and(m, 3) == jnp.bitwise_and(n, 3))
    xi, xi_twice = entries(m, n, (first, twice))
    eta, eta_twice = entries(jnp.right_shift(m, 2), jnp.right_shift(n, 2), (first, twice))
    parts = [
        jnp.where(same_row, xi, 0.0),
        jnp.where(same_column, eta, 0.0),
        jnp.where(same_row, xi_twice, 0.0) + jnp.where(same_column, eta_twice, 0.0),
    ]
    return split(jnp.concatenate(parts, axis=1))


def split(values):
    high = values.astype(BF)
    low = (values - high.astype(F32)).astype(BF)
    return high, low


def dot(a, b):
    return jnp.dot(a, b, preferred_element_type=F32)


def dot_nt(a, b):
    return lax.dot_general(a, b, (((1,), (1,)), ((), ())), preferred_element_type=F32)


def lane_pick(chunk_of, chunks, index):
    low = jnp.bitwise_and(index, LANES - 1)
    high = jnp.right_shift(index, 7)
    total = jnp.zeros(index.shape, F32)
    for at in range(chunks):
        row = jnp.broadcast_to(chunk_of(at), index.shape)
        picked = jnp.take_along_axis(row, low, axis=1, mode="promise_in_bounds")
        total = jnp.where(high == at, picked, total)
    return total


def out_kernel(surface, table, weight, payload):
    atmos = lax.axis_index("comp") != lax.axis_size("comp") - 1
    fields = surface.shape[0]
    chunks = surface.shape[2] // LANES

    @pl.when(atmos)
    def _():
        source = table[:, 0, :]
        for f in range(fields):
            rows_of = lambda at: surface[f, 0:1, at * LANES : (at + 1) * LANES]
            payload[:, f, :] = lane_pick(rows_of, chunks, source) * weight[...]
        payload[:, fields, :] = table[:, 1, :].astype(F32)

    @pl.when(jnp.logical_not(atmos))
    def _():
        payload[...] = jnp.zeros(payload.shape, F32)
        for f in range(fields):
            for at in range(chunks):
                payload[at, f : f + 1, :] = surface[f, 0:1, at * LANES : (at + 1) * LANES]


def back_kernel(got0, got1, got2, table, weight, after, payload):
    comp = lax.axis_index("comp")
    fields = got0.shape[1] - 1
    chunks = 16
    wide = fields + 1

    @pl.when(comp != 3)
    def _():
        source = table[:, 0, :]
        scale = weight[...]
        for f in range(fields):

            def pick(at):
                first, second, third = (got[at, f : f + 1, :] for got in (got0, got1, got2))
                return jnp.where(comp == 0, first, jnp.where(comp == 1, second, third))

            rows = lane_pick(pick, chunks, source)
            payload[:, f, :] = rows * scale
        payload[:, fields, :] = table[:, 1, :].astype(F32)
        payload[:, wide:, :] = jnp.zeros((payload.shape[0], payload.shape[1] - wide, LANES), F32)

    @pl.when(comp == 3)
    def _():
        payload[:, 0:wide, :] = got0[...]
        payload[:, wide : 2 * wide, :] = got1[...]
        payload[:, 2 * wide : 3 * wide, :] = got2[...]


def pick_rims(wanted, parts):
    nodes = parts.shape[1]
    rows = parts.shape[0] // 2
    many = wanted.shape[1]
    ids = lax.broadcasted_iota(jnp.int16, (nodes, many), 0)
    wanted = jnp.broadcast_to(wanted, (16, many)).astype(jnp.int16)
    wanted = jnp.broadcast_to(wanted[None], (nodes // 16, 16, many)).reshape(nodes, many)
    onehot = jnp.where(ids == wanted, jnp.ones((), BF), jnp.zeros((), BF))
    both = dot(parts[...], onehot)
    return both[:rows] + both[rows:]


def count_links(index, order, target):
    width = target.shape[1]
    one = jnp.ones((16, width), BF)
    zero = jnp.zeros((16, width), BF)
    ids = lax.broadcasted_iota(jnp.int16, (16, width), 0)
    low_off = [
        jnp.broadcast_to(jnp.bitwise_and(row, LANES - 1), (16, width)).astype(jnp.int16) - ids for row in index
    ]
    highs = [jnp.broadcast_to(jnp.right_shift(row, 7), (16, width)).astype(BF) for row in index]
    masks = [[jnp.where(high == block, one, zero) for high in highs] for block in order]
    for sub in range(LANES // 16):
        lows = [jnp.where(off == sub * 16, one, zero) for off in low_off]
        for slot in range(len(order)):
            total = None
            for low, mask in zip(lows, masks[slot]):
                term = low * mask
                total = term if total is None else total + term
            target[slot * LANES + sub * 16 : slot * LANES + sub * 16 + 16, :] = total

def gain_of(ocean, number, metric):
    return OCEAN_RATE * metric if ocean else ATM_STEP / (1.0 + number)

def atmos_field(values, scale, table_high, table_low):
    third = values.shape[0] // 3
    high, low = split(values)
    grads = dot(jnp.concatenate([high, low], axis=1), table_high) + dot(high, table_low)
    grad_xi = grads[:, :LANES]
    grad_eta = grads[:, LANES : 2 * LANES]
    second = grads[:, 2 * LANES :]
    wind_u = jnp.concatenate([values[:third]] * 3, axis=0)
    wind_v = jnp.concatenate([values[third : 2 * third]] * 3, axis=0)
    return (VISCOSITY * scale * scale) * second - scale * (wind_u * grad_xi + wind_v * grad_eta)


def fill_parts(atmos, state, metric, parts, tables):
    rows, nodes = state.shape

    @pl.when(atmos)
    def _():
        high, low = derivative_table()
        tables[:LANES, :] = high
        tables[LANES : 2 * LANES, :] = high
        tables[2 * LANES :, :] = low
        for at in range(nodes // LANES):
            where = slice(at * LANES, (at + 1) * LANES)
            field = atmos_field(state[:, where], metric[0:1, where], tables[: 2 * LANES, :], tables[2 * LANES :, :])
            high, low = split(field)
            parts[0:rows, where] = high
            parts[rows:, where] = low

    @pl.when(jnp.logical_not(atmos))
    def _():
        high, low = split(state[...])
        parts[0:rows, :] = high
        parts[rows:, :] = low


def field_kernel(state, metric, rims, state_here, left_ref, right_ref, parts, tables):
    state_here[...] = state[...]
    fill_parts(lax.axis_index("comp") != lax.axis_size("comp") - 1, state, metric, parts, tables)
    rim = rims.shape[1]
    sides = pick_rims(jnp.concatenate([rims[0:1, :], rims[1:2, :]], axis=1), parts)
    left_ref[...] = sides[:, :rim]
    right_ref[...] = sides[:, rim:]


def inner_kernel(state, metric, links, column, after, partial, gains, links_out, column_out, count, parts, tables):
    atmos = lax.axis_index("comp") != lax.axis_size("comp") - 1
    rows, nodes = state.shape
    unroll, _, width = count.shape
    chunks = nodes // LANES
    column_out[...] = column[...]
    links_out[...] = links[...]
    fill_parts(atmos, state, metric, parts, tables)

    def run(used, is_ocean):
        def step(at, here):
            where = pl.ds(pl.multiple_of(at * width, width), width)
            index = [links[k, :, where] for k in range(used)]
            number = sum((row >= 0).astype(F32) for row in index)
            count_links(index, list(range(1, chunks + 1)), here)
            both = dot(parts[...], here[...])
            linked = both[:rows] + both[rows:]
            current = state[:, where]
            gain = gain_of(is_ocean, number, metric[0:1, where])
            gains[0:1, where] = gain
            if is_ocean:
                partial[:, where] = current + gain * (linked - number * current)
            else:
                field = parts[0:rows, where].astype(F32) + parts[rows:, where].astype(F32)
                partial[:, where] = current + gain * (field + linked)

        def group(i, carry):
            for u in range(unroll):
                step(i * unroll + u, count.at[u])
            return carry

        lax.fori_loop(0, nodes // width // unroll, group, 0)

    @pl.when(atmos)
    def _():
        run(3, False)

    @pl.when(jnp.logical_not(atmos))
    def _():
        run(6, True)


def rim_kernel(partial, left, right, gains, links, column, mixed, column_out, rim_parts, count, wide):
    comp = lax.axis_index("comp")
    tile = lax.axis_index("tile")
    last_comp = lax.axis_size("comp") - 1
    last_tile = lax.axis_size("tile") - 1
    ocean = comp == last_comp
    has_left = jnp.logical_not((tile == 0) & (ocean | (comp == 0)))
    has_right = jnp.logical_not((tile == last_tile) & (comp >= last_comp - 1))
    rows, nodes = partial.shape
    levels = column.shape[0]
    rim = left.shape[1]
    width = 2 * LANES
    chunks = nodes // LANES
    column_out[...] = column[...]
    for side, there, source in ((0, has_left, left), (1, has_right, right)):
        high, low = split(jnp.where(there, source[...], 0.0))
        rim_parts[0:rows, side * rim : (side + 1) * rim] = high
        rim_parts[rows:, side * rim : (side + 1) * rim] = low
    wide[...] = jnp.zeros(wide.shape, F32)
    for f in range(rows // levels):
        at = f * levels
        wide[at : at + levels, at : at + levels] = column[...]
    col_high, col_low = split(wide[:, 0:rows])
    col = jnp.concatenate([col_high, col_low], axis=0)

    def run(used):
        for at in range(nodes // width):
            where = slice(at * width, (at + 1) * width)
            here = count.at[at % 2]
            count_links([links[k, :, where] for k in range(used)], [0, chunks + 1], here)
            both = dot(rim_parts[...], here[...])
            updated = partial[:, where] + gains[0:1, where] * (both[:rows] + both[rows:])
            high, low = split(updated)
            full = dot(col, high)
            mixed[:, where] = full[:rows] + full[rows:] + dot(col_high, low)

    @pl.when(jnp.logical_not(ocean))
    def _():
        run(3)

    @pl.when(ocean)
    def _():
        run(6)


def final_kernel(mixed, got, column, result, done, left_rows, onehots, sems):
    last_comp = lax.axis_size("comp") - 1
    ocean = lax.axis_index("comp") == last_comp
    rows, nodes = mixed.shape
    levels = column.shape[0]
    senders = got.shape[0]
    width = 2 * LANES
    tiles = nodes // width
    fields = rows // levels
    chunks = nodes // LANES
    ids = lax.broadcasted_iota(jnp.int16, (LANES, LANES), 0)
    ids_high = lax.broadcasted_iota(jnp.int16, (chunks, LANES), 0)
    one = jnp.ones((), BF)
    zero = jnp.zeros((), BF)

    def land(part, total):
        for a in range(senders):
            base_row = 4 * part
            cell = got[a, pl.ds(base_row + fields, 1), :].astype(jnp.int32)
            lane_low = jnp.broadcast_to(jnp.bitwise_and(cell, LANES - 1), (chunks, LANES)).astype(jnp.int16)
            lane_high = jnp.broadcast_to(jnp.right_shift(cell, 7), (chunks, LANES)).astype(jnp.int16)
            wanted = jnp.broadcast_to(lane_low[None], (LANES // chunks, chunks, LANES)).reshape(LANES, LANES)
            where = slice(a * LANES, (a + 1) * LANES)
            onehots[:, where] = jnp.where(ids == wanted, one, zero)
            mask = ids_high == lane_high
            for f in range(fields):
                row = got[a, pl.ds(base_row + f, 1), :]
                high = row.astype(BF).astype(F32)
                for n, value in ((f, high), (fields + f, row - high)):
                    spread = jnp.broadcast_to(value, (chunks, LANES)).astype(BF)
                    left_rows[n * chunks : (n + 1) * chunks, where] = jnp.where(mask, spread, zero)
        return total + dot_nt(left_rows[...], onehots[...])

    groups = jnp.where(ocean, last_comp, 1)
    landed = lax.fori_loop(0, groups, land, jnp.zeros((2 * fields * chunks, LANES), F32))
    forcing = COUPLING * (landed[: fields * chunks] + landed[fields * chunks :])

    col_gain = jnp.broadcast_to(column[:, 0:1], (levels, width))

    def move(at):
        where = pl.ds(at * width, width)
        return pltpu.make_async_copy(done.at[:, where], result.at[:, where], sems.at[at])

    for at in range(tiles):
        where = slice(at * width, (at + 1) * width)
        for f in range(fields):
            part = slice(f * levels, (f + 1) * levels)
            first = f * chunks + at * width // LANES
            rows_of = [forcing[n : n + 1, :] for n in range(first, first + width // LANES)]
            done[part, where] = mixed[part, where] + col_gain * jnp.concatenate(rows_of, axis=1)
        move(at).start()

    for at in range(tiles):
        move(at).wait()


def call(kernel, args, outs, scratch=(), limit=32, form="vmem", anywhere=(), out_far=(), cost=None, alias=None):
    free = pl.BlockSpec(memory_space=pl.ANY)
    whole = pl.BlockSpec(memory_space=pltpu.VMEM)

    def spec(dims):
        if form == "block":
            return pl.BlockSpec(dims, lambda i: (0,) * len(dims))
        return free if form == "any" else whole

    params = pltpu.CompilerParams() if limit is None else pltpu.CompilerParams(vmem_limit_bytes=limit * MIB)
    return pl.pallas_call(
        kernel,
        grid=(1,) if form == "block" else (),
        in_specs=[free if n in anywhere else spec(arg.shape) for n, arg in enumerate(args)],
        out_specs=[free if n in out_far else spec(out.shape) for n, out in enumerate(outs)],
        out_shape=outs,
        scratch_shapes=list(scratch),
        compiler_params=params,
        input_output_aliases=alias or {},
        cost_estimate=cost and pl.CostEstimate(flops=cost, bytes_accessed=4_000_000, transcendentals=0),
    )(*args)


def per_device(state, metric, column_op, links, rims, out_map, out_weight, back_map, back_weight):
    _, _, fields, levels, nodes = state.shape
    rows = fields * levels
    rim = rims.shape[-1]
    ntile = lax.axis_size("tile")
    ncomp = lax.axis_size("comp")
    slot = out_map.shape[-1]
    axes = ("comp", "tile")
    total = ncomp * ntile
    chunks = nodes // LANES
    width = 2 * LANES
    tiles = nodes // width
    metric_row = metric.reshape(1, nodes)
    link_rows = links.reshape(6, 1, nodes)
    dma = pltpu.SemaphoreType.DMA
    int32 = jnp.int32

    def shape(*dims, kind=F32):
        return jax.ShapeDtypeStruct(dims, kind)

    def held(*dims, kind=F32):
        return pltpu.VMEM(dims, kind)

    (payload,) = pl.pallas_call(
        out_kernel,
        grid=(1,),
        in_specs=[
            pl.BlockSpec((fields, 8, nodes), lambda i: (0, 0, 0)),
            pl.BlockSpec((ntile, 2, slot), lambda i: (0, 0, 0)),
            pl.BlockSpec((ntile, slot), lambda i: (0, 0)),
        ],
        out_specs=[pl.BlockSpec((ntile, fields + 1, slot), lambda i: (0, 0, 0))],
        out_shape=[shape(ntile, fields + 1, slot)],
    )(state.reshape(fields, levels, nodes), out_map.reshape(ntile, 2, slot), out_weight.reshape(ntile, slot))

    def across(values, flip):
        pairs = [(a * ntile + b, (a ^ flip) * ntile + b) for a in range(ncomp) for b in range(ntile)]
        return lax.ppermute(values, axes, pairs)

    got0 = across(payload, 3)
    got1 = across(payload, 2)
    got2 = across(payload, 1)

    current = state.reshape(rows, nodes)
    state_here, to_left, to_right = call(
        field_kernel,
        (current, metric_row, rims.reshape(2, rim)),
        [shape(rows, nodes), shape(rows, rim), shape(rows, rim)],
        [held(2 * rows, nodes, kind=BF), held(3 * LANES, 3 * LANES, kind=BF)],

        cost=4_000_000_000,
    )
    steps = [(i, (i + 1) % total) for i in range(total)]
    left = lax.ppermute(to_right, axes, steps)
    right = lax.ppermute(to_left, axes, [(b, a) for a, b in steps])
    (rows_out,) = call(
        back_kernel,
        (got0, got1, got2, back_map.reshape(ntile, 2, slot), back_weight.reshape(ntile, slot), to_right),
        [shape(ntile, (ncomp - 1) * (fields + 1), slot)],
        anywhere=(5,),
    )
    got = lax.all_to_all(rows_out, "tile", split_axis=0, concat_axis=0, tiled=True)

    partial, gains, links_here, column = call(
        inner_kernel,
        (state_here, metric_row, link_rows, column_op.reshape(levels, levels), rows_out),
        [shape(rows, nodes), shape(1, nodes), shape(6, 1, nodes, kind=int32), shape(levels, levels)],
        [held(4, nodes, width, kind=BF), held(2 * rows, nodes, kind=BF), held(3 * LANES, 3 * LANES, kind=BF)],
        anywhere=(4,),
        cost=8_000_000_000,
        alias={0: 0},
    )
    mixed, column = call(
        rim_kernel,
        (partial, left, right, gains, links_here, column),
        [shape(rows, nodes), shape(levels, levels)],
        [held(2 * rows, 2 * rim, kind=BF), held(2, 2 * rim, width, kind=BF), held(rows, width)],
        alias={0: 0},
    )
    (result,) = call(
        final_kernel,
        (mixed, got, column),
        [shape(rows, nodes)],
        [
            held(rows, nodes),
            held(2 * fields * chunks, ntile * slot, kind=BF),
            held(LANES, ntile * slot, kind=BF),
            dma((tiles,)),
        ],
        out_far=(0,),
    )
    return result.reshape(state.shape)


def solution(mesh):
    return jax.shard_map(
        per_device,
        mesh=mesh,
        in_specs=(
            P("comp", "tile", None, None, None),
            P("comp", "tile", None),
            P("comp", None, None),
            P("comp", "tile", None, None),
            P("comp", "tile", None, None),
            P("comp", "tile", None, None, None),
            P("comp", "tile", None, None),
            P("comp", "tile", None, None, None),
            P("comp", "tile", None, None),
        ),
        out_specs=P("comp", "tile", None, None, None),
        check_vma=False,
    )
```
